512 devices in a mesh: row: 32 (over z, core), col: 16 (over x, y).
Axes of the slice: x: 4, y: 4, z: 16, core: 2. Of those that a mesh axis runs over, the one named last changes fastest.
Arguments:
- panel_t: float32 [256, 131072], P('col', 'row'), may hold values from -1 to 1
- trailing: float32 [131072, 2048], P('row', 'col'), may hold values from -6 to 6
Outputs:
- r_factor: float32 [256, 256], replicated
- top_rows: float32 [256, 2048], P(None, 'col')
- updated: float32 [131072, 2048], P('row', 'col')
The draws below stay inside these ranges and needn't reach their ends.
All inputs are finite; a program needn't handle non-finite values.
Results may differ from the reference program's by a relative error of at most 0.00011.
Values sent between devices are 32-bit elements; how exact they have to be, the bound alone decides.
A program may use at most 128 MiB of HBM per device.

```python
import math
import jax
import jax.numpy as jnp
from jax import lax

NB = 256
NT = 2048
M = 131072


def draw_panel_t(key, part):
    key = jax.random.fold_in(key, 11)
    base_key = jax.random.fold_in(key, 0)
    base = jnp.clip(jax.random.normal(base_key, (NB + 1, M), jnp.float32), -6.0, 6.0)
    blended = base[1:] + 0.6 * base[:-1]
    return blended * (1.0 / math.sqrt(M))


def block_scale(rng, shape, cuts, least, high):
    gain = 1.0
    for position, parts in cuts:
        draws = jax.random.uniform(jax.random.fold_in(jax.random.fold_in(rng, 6), position), (parts,), jnp.float32, least / len(cuts), high / len(cuts))
        gain = gain * jnp.repeat(jnp.exp(draws), shape[position] // parts).reshape((-1,) + (1,) * (len(shape) - 1 - position))
    return gain


def normal_values(key, dims, scale, bound, shards=(), held_as=jnp.bfloat16):
    entries = scale * jax.random.normal(key, dims, jnp.float32)
    if shards:
        entries = entries * block_scale(key, dims, shards, -0.22, 0.18)
    return jnp.clip(entries, -bound, bound).astype(held_as)


def setup_inputs(seed: int = 0) -> dict:
    arg_keys = jax.random.split(jax.random.key(seed), 3)
    return {
        "panel_t": draw_panel_t(jax.random.fold_in(arg_keys[2], 71), 0),
        "trailing": normal_values(arg_keys[1], (M, NT), 1.0, 6.0, ((0, 32), (1, 16)), jnp.float32),
    }


HIGHEST = lax.Precision.HIGHEST

def reference(panel_t, trailing):
    gram = lax.dot_general(panel_t.astype(jnp.float32), panel_t.astype(jnp.float32), (((1,), (1,)), ((), ())), precision=HIGHEST, preferred_element_type=jnp.float32)
    lower_factor = jnp.linalg.cholesky(gram)
    projection = jnp.dot(panel_t.astype(jnp.float32), trailing.astype(jnp.float32), precision=HIGHEST, preferred_element_type=jnp.float32)
    top_rows = lax.linalg.triangular_solve(lower_factor, projection, left_side=True, lower=True)
    coeffs = lax.linalg.triangular_solve(lower_factor, top_rows, left_side=True, lower=True, transpose_a=True)
    change = lax.dot_general(panel_t.astype(jnp.float32), coeffs.astype(jnp.float32), (((0,), (0,)), ((), ())), precision=HIGHEST, preferred_element_type=jnp.float32)
    return (lower_factor.T, top_rows, trailing - change)
```

```python
import jax
import jax.numpy as jnp
from jax import lax
from jax.experimental import pallas as pl
from jax.experimental.pallas import tpu as pltpu
from jax.sharding import PartitionSpec as P

MESH = pl.DeviceIdType.MESH
K = 4096
H = K // 2
S1P, S1M, F1P, F1M = 0, 1, 2, 3
S2P, S2M, F2P, F2M = 4, 9, 14, 18
NMSG = 22

class Half:
    def __init__(self, half, panel, g, ssem, rsem, x, y):
        self.h, self.panel, self.g, self.ss, self.rs = half, panel, g, ssem, rsem
        self.p, self.q = (x, y) if half == 0 else (y, x)
        w = lambda v: lax.rem(v, 4)
        self.P = [self.p, w(self.p + 3), w(self.p + 1), w(self.p + 2)]
        self.Q = [self.q, w(self.q + 3), w(self.q + 1), w(self.q + 2)]
        self.pending = []
    def col(self, p, q):
        return p * 4 + q if self.h == 0 else q * 4 + p
    def slc(self, p, q, lo, n):
        r = pl.multiple_of(self.col(p, q) * 16 + 8 * self.h, 8)
        return self.g.at[pl.ds(r, 8), pl.ds(lo, n)]
    def send(self, m, p, q, lo, n, axis, sign, own=False):
        dst = self.slc(p, q, lo, n)
        src = self.panel.at[pl.ds(8 * self.h, 8), pl.ds(lo, n)] if own else dst
        i = 1 if sign < 0 else 2
        to = self.col(self.P[i], self.q) if axis == 1 else self.col(self.p, self.Q[i])
        c = pltpu.make_async_remote_copy(src, dst, self.ss.at[self.h, m], self.rs.at[self.h, m], device_id={"col": to}, device_id_type=MESH)
        c.start()
        self.pending.append(c)
    def recv(self, m, p, q, lo, n):
        d = self.slc(p, q, lo, n)
        pltpu.make_async_remote_copy(d, d, self.ss.at[self.h, m], self.rs.at[self.h, m], device_id={"col": self.col(self.P[1], self.q)}, device_id_type=MESH).wait_recv()
    def start_own(self):
        self.send(S1P, self.p, self.q, 0, K, 1, 1, True)
        self.send(S1M, self.p, self.q, 0, K, 1, -1, True)
    def start_own2(self):
        self.send(S2P, self.p, self.q, 0, K, 2, 1, True)
        self.send(S2M, self.p, self.q, 0, K, 2, -1, True)
    def first_p(self):
        pm = self.P[1]
        self.recv(S1P, pm, self.q, 0, K)
        self.send(F1P, pm, self.q, 0, H, 1, 1)
        self.send(S2P + 1, pm, self.q, 0, K, 2, 1)
        self.send(S2M + 1, pm, self.q, 0, K, 2, -1)
    def first_m(self):
        pp = self.P[2]
        self.recv(S1M, pp, self.q, 0, K)
        self.send(F1M, pp, self.q, H, H, 1, -1)
        self.send(S2P + 2, pp, self.q, 0, K, 2, 1)
        self.send(S2M + 2, pp, self.q, 0, K, 2, -1)
    def far(self):
        po = self.P[3]
        self.recv(F1P, po, self.q, 0, H)
        self.send(S2P + 3, po, self.q, 0, H, 2, 1)
        self.send(S2M + 3, po, self.q, 0, H, 2, -1)
        self.recv(F1M, po, self.q, H, H)
        self.send(S2P + 4, po, self.q, H, H, 2, 1)
        self.send(S2M + 4, po, self.q, H, H, 2, -1)
    def second(self, s):
        ps = self.P[s]
        if s < 3:
            self.recv(S2P + s, ps, self.Q[1], 0, K)
            self.send(F2P + s, ps, self.Q[1], 0, H, 2, 1)
            self.recv(S2M + s, ps, self.Q[2], 0, K)
            self.send(F2M + s, ps, self.Q[2], H, H, 2, -1)
        else:
            self.recv(S2P + 3, ps, self.Q[1], 0, H)
            self.send(F2P + 3, ps, self.Q[1], 0, H, 2, 1)
            self.recv(S2M + 3, ps, self.Q[2], 0, H)
            self.recv(S2P + 4, ps, self.Q[1], H, H)
            self.recv(S2M + 4, ps, self.Q[2], H, H)
            self.send(F2M + 3, ps, self.Q[2], H, H, 2, -1)
    def last(self, s):
        ps, qo = self.P[s], self.Q[3]
        self.recv(F2P + s, ps, qo, 0, H)
        self.recv(F2M + s, ps, qo, H, H)


HI = lax.Precision.HIGHEST
NC = 16

def dot(a, b, ca=1, cb=0):
    return lax.dot_general(a, b, (((ca,), (cb,)), ((), ())), precision=HI, preferred_element_type=jnp.float32)

def rcopy(src, dst, ss, rs, **dev):
    return pltpu.make_async_remote_copy(src, dst, ss, rs, device_id=dev, device_id_type=MESH)

def make_kernel(NR):
    NZ = NR // 2
    PW = 32 // NR
    PZ = 128 // NZ
    def kernel(panel, trail, g, psum, gram, ssem, rsem, lsem, xb, gp, rs16, gs, rs32, ga, gall, pp, pex, prs, pown, qs, qr):
        c = lax.axis_index("col")
        w = lax.axis_index("row")
        x, y = c // 4, lax.rem(c, 4)
        z, core = w // 2, lax.rem(w, 2)
        sib = z * 2 + 1 - core
        own = pltpu.make_async_copy(panel, g.at[pl.ds(pl.multiple_of(c * 16, 16), 16), :], lsem.at[0])
        own.start()
        mine = pltpu.make_async_copy(panel.at[:, pl.ds(pl.multiple_of(c * 256, 256), 256)], xb.at[pl.ds(pl.multiple_of(c * 16, 16), 16), :], lsem.at[1])
        mine.start()
        A = Half(0, panel, g, ssem, rsem, x, y)
        B = Half(1, panel, g, ssem, rsem, x, y)
        bar = pltpu.get_barrier_semaphore()
        for i in range(1, NC):
            pl.semaphore_signal(bar, inc=1, device_id={"col": lax.rem(c + i, NC)}, device_id_type=MESH)
        for i in range(1, NR):
            pl.semaphore_signal(bar, inc=1, device_id={"row": lax.rem(w + i, NR)}, device_id_type=MESH)
        pl.semaphore_wait(bar, NC + NR - 2)
        for i in range(1, NC):
            j = lax.rem(c + i, NC)
            rcopy(panel.at[:, pl.ds(pl.multiple_of(j * 256, 256), 256)], xb.at[pl.ds(pl.multiple_of(c * 16, 16), 16), :], qs.at[0], qr.at[0], col=j).start()
        A.start_own(); B.start_own(); A.start_own2(); B.start_own2()
        def wait_bytes(ref, k, send):
            d = rcopy(ref, ref, qs.at[k], qr.at[k], col=lax.rem(c + 1, NC))
            d.wait_send() if send else d.wait_recv()
        mine.wait()
        wait_bytes(xb.at[pl.ds(0, 240), :], 0, False)
        xv = xb[...]
        gp[...] = dot(xv, xv, 1, 1)
        for i in range(1, NC):
            j = lax.rem(c + i, NC)
            rcopy(gp.at[pl.ds(pl.multiple_of(j * 16, 16), 16), :], rs16.at[i - 1], qs.at[1], qr.at[1], col=j).start()
        A.first_p(); B.first_p(); A.first_m(); B.first_m()
        wait_bytes(rs16, 1, False)
        acc = gp[pl.ds(pl.multiple_of(c * 16, 16), 16), :]
        for i in range(NC - 1):
            acc = acc + rs16[i]
        for h in range(2):
            for r in range(16):
                gs[h * 16 + r] = acc[r:r + 1, 128 * h:128 * h + 128]
        for i in range(1, NR):
            j = lax.rem(w + i, NR)
            rcopy(gs.at[pl.ds(j * PW, PW)], rs32.at[pl.ds((i - 1) * PW, PW)], qs.at[2], qr.at[2], row=j).start()
        A.second(0); B.second(0)
        wait_bytes(rs32, 2, False)
        tot = gs[pl.ds(w * PW, PW)]
        for i in range(NR - 1):
            tot = tot + rs32[pl.ds(i * PW, PW)]
        ga[pl.ds(w * PW, PW)] = tot
        for i in range(1, NR):
            j = lax.rem(w + i, NR)
            rcopy(ga.at[pl.ds(w * PW, PW)], ga.at[pl.ds(w * PW, PW)], qs.at[3], qr.at[3], row=j).start()
        A.far(); B.far()
        wait_bytes(ga.at[pl.ds(0, 32 - PW)], 3, False)
        for i in range(1, NC):
            j = lax.rem(c + i, NC)
            rcopy(ga, gall.at[c], qs.at[4], qr.at[4], col=j).start()
        gall[c] = ga[...]
        for s in (1, 2, 3):
            A.second(s); B.second(s)
        wait_bytes(gall.at[pl.ds(0, 15)], 4, False)
        for b in range(NC):
            for h in range(2):
                for t in range(2):
                    gram[16 * b + 8 * t:16 * b + 8 * t + 8, 128 * h:128 * h + 128] = gall[b, 16 * h + 8 * t:16 * h + 8 * t + 8, 0, :]
        for s in range(4):
            A.last(s); B.last(s)
        own.wait()
        pp[...] = jnp.zeros_like(pp)
        CH = 512
        @pl.loop(0, K // CH)
        def _(i):
            k0 = pl.multiple_of(i * CH, CH)
            pp[...] += dot(g[:, pl.ds(k0, CH)], trail[pl.ds(k0, CH), :])
        ex = rcopy(pp.at[pl.ds(pl.multiple_of((1 - core) * 128, 128), 128), :], pex, qs.at[5], qr.at[5], row=sib)
        ex.start(); ex.wait_recv()
        pex[...] += pp[pl.ds(pl.multiple_of(core * 128, 128), 128), :]
        for i in range(1, NZ):
            j = lax.rem(z + i, NZ)
            rcopy(pex.at[pl.ds(pl.multiple_of(j * PZ, PZ), PZ), :], prs.at[pl.ds((i - 1) * PZ, PZ), :], qs.at[6], qr.at[6], row=j * 2 + core).start()
        wait_bytes(prs, 6, False)
        tot = pex[pl.ds(pl.multiple_of(z * PZ, PZ), PZ), :]
        for i in range(NZ - 1):
            tot = tot + prs[i * PZ:(i + 1) * PZ, :]
        me = pl.multiple_of(core * 128 + z * PZ, PZ)
        psum[pl.ds(me, PZ), :] = tot
        for i in range(1, NZ):
            j = lax.rem(z + i, NZ)
            rcopy(psum.at[pl.ds(me, PZ), :], psum.at[pl.ds(me, PZ), :], qs.at[7], qr.at[7], row=j * 2 + core).start()
        wait_bytes(psum.at[pl.ds(0, 128 - PZ), :], 7, False)
        half = psum.at[pl.ds(pl.multiple_of(core * 128, 128), 128), :]
        back = rcopy(half, half, qs.at[8], qr.at[8], row=sib)
        back.start(); back.wait_recv()
        for q in A.pending + B.pending:
            q.wait_send()
        wait_bytes(xb.at[pl.ds(0, 240), :], 0, True)
        wait_bytes(rs16, 1, True)
        wait_bytes(rs32, 2, True)
        wait_bytes(ga.at[pl.ds(0, 32 - PW)], 3, True)
        wait_bytes(gall.at[pl.ds(0, 15)], 4, True)
        ex.wait_send()
        wait_bytes(prs, 6, True)
        wait_bytes(psum.at[pl.ds(0, 128 - PZ), :], 7, True)
        back.wait_send()
    f32 = jnp.float32
    V = pl.BlockSpec(memory_space=pltpu.VMEM)
    def call(panel, trail):
        return pl.pallas_call(kernel,
            out_shape=[jax.ShapeDtypeStruct((256, K), f32), jax.ShapeDtypeStruct((256, 128), f32), jax.ShapeDtypeStruct((256, 256), f32)],
            in_specs=[pl.BlockSpec(memory_space=pl.ANY), V], out_specs=[V, V, V],
            scratch_shapes=[pltpu.SemaphoreType.DMA((2, NMSG)), pltpu.SemaphoreType.DMA((2, NMSG)), pltpu.SemaphoreType.DMA((2,)),
                pltpu.VMEM((256, 256), f32), pltpu.VMEM((256, 256), f32), pltpu.VMEM((15, 16, 256), f32),
                pltpu.VMEM((32, 1, 128), f32), pltpu.VMEM((PW * (NR - 1), 1, 128), f32), pltpu.VMEM((32, 1, 128), f32), pltpu.VMEM((16, 32, 1, 128), f32),
                pltpu.VMEM((256, 128), f32), pltpu.VMEM((128, 128), f32), pltpu.VMEM((PZ * (NZ - 1), 128), f32), pltpu.VMEM((8, 128), f32),
                pltpu.SemaphoreType.DMA((9,)), pltpu.SemaphoreType.DMA((9,))],
            compiler_params=pltpu.CompilerParams(collective_id=0, has_side_effects=True, vmem_limit_bytes=50 << 20))(panel, trail)
    return call

T = 8
N = 128

def factor_half(tiles):
    n = len(tiles)
    sub = lax.broadcasted_iota(jnp.int32, (T, N), 0)
    lane = lax.broadcasted_iota(jnp.int32, (T, N), 1)
    bl = lambda x, c: jnp.broadcast_to(x[:, c:c + 1], (T, N))
    bs = lambda x, r: jnp.broadcast_to(x[r:r + 1, :], (T, N))
    tiles = list(tiles)
    Rs, Ls = [], []
    for k in range(n):
        t = tiles[k]
        inb = (lane >= T * k) & (lane < T * k + T)
        eye = jnp.where(lane - T * k == sub, 1.0, 0.0)
        cols = [bl(t, T * k + m) for m in range(T)]
        z = jnp.where(inb, eye, t)
        u = t
        li = z
        dinv = jnp.zeros((T, N), jnp.float32)
        drs = jnp.zeros((T, N), jnp.float32)
        for j in range(T):
            piv = bs(cols[j], j)
            r = 1.0 / piv
            f = jnp.where(sub == j, 0.0, cols[j] * r)
            fl = jnp.where(sub > j, f, 0.0)
            for m in range(j + 1, T):
                cols[m] = cols[m] - f * bs(cols[m], j)
            dinv = jnp.where(sub == j, r, dinv)
            drs = jnp.where(sub == j, lax.rsqrt(piv), drs)
            z = z - f * bs(z, j)
            u = u - fl * bs(u, j)
            li = li - fl * bs(li, j)
        z = z * dinv
        row = sub + T * k
        Rs.append(jnp.where(lane >= row, u * drs, 0.0))
        Ls.append(jnp.where(lane <= row, li * drs, 0.0))
        zr = [bs(z, m) for m in range(T)]
        for i in range(k + 1, n):
            ti = tiles[i]
            c = [bl(ti, T * k + m) for m in range(T)]
            p = [c[m] * zr[m] for m in range(T)]
            while len(p) > 1:
                p = [p[a] + p[a + 1] for a in range(0, len(p), 2)]
            tiles[i] = jnp.where(inb, 0.0, ti) - p[0]
    return Rs, Ls


CH = 512
def finish(gram, psum, g, trail, r_ref, top_ref, out, li_ref):
    h = N
    def half(read, ro):
        R, L = factor_half([read(i) for i in range(16)])
        for i in range(16):
            r_ref[ro + 8 * i: ro + 8 * i + 8, ro:ro + h] = R[i]
            li_ref[ro + 8 * i: ro + 8 * i + 8, ro:ro + h] = L[i]
    @pl.when(pl.program_id(0) == 0)
    def _():
        half(lambda i: gram[8 * i:8 * i + 8, :h], 0)
        linv1 = li_ref[:h, :h]
        r12 = dot(linv1, gram[:h, h:])
        r_ref[:h, h:] = r12
        r_ref[h:, :h] = jnp.zeros((h, h), jnp.float32)
        li_ref[:h, h:] = jnp.zeros((h, h), jnp.float32)
        s = gram[h:, h:] - dot(r12, r12, 0, 0)
        half(lambda i: s[8 * i:8 * i + 8, :], h)
        t = dot(r12, linv1, 0, 0)
        li_ref[h:, :h] = -dot(li_ref[h:, h:], t)
        top_ref[...] = dot(li_ref[...], psum[...])
        psum[...] = dot(li_ref[...], top_ref[...], 0, 0)
    out[...] = trail[...] - dot(g[...], psum[...], 0, 0)

def finish_call(gram, psum, g, trail):
    f32 = jnp.float32
    W = lambda s: pl.BlockSpec(s, lambda i: (0, 0))
    def kk(gram, psum_in, g, trail, r_ref, top_ref, out, li_ref, cf):
        @pl.when(pl.program_id(0) == 0)
        def _():
            cf[...] = psum_in[...]
        finish(gram, cf, g, trail, r_ref, top_ref, out, li_ref)
    return pl.pallas_call(kk, grid=(K // CH,),
        in_specs=[W((256, 256)), W((256, 128)), pl.BlockSpec((256, CH), lambda i: (0, i)), pl.BlockSpec((CH, 128), lambda i: (i, 0))],
        out_specs=[W((256, 256)), W((256, 128)), pl.BlockSpec((CH, 128), lambda i: (i, 0))],
        out_shape=[jax.ShapeDtypeStruct((256, 256), f32), jax.ShapeDtypeStruct((256, 128), f32), jax.ShapeDtypeStruct((K, 128), f32)],
        scratch_shapes=[pltpu.VMEM((256, 256), f32), pltpu.VMEM((256, 128), f32)],
        compiler_params=pltpu.CompilerParams(vmem_limit_bytes=40 << 20))(gram, psum, g, trail)

def solution(mesh):
    k=make_kernel(mesh.shape["row"])
    def body(panel, trail):
        g, ps, gram = k(panel, trail)
        return tuple(finish_call(gram, ps, g, trail))
    return jax.shard_map(body, mesh=mesh, in_specs=(P("col","row"),P("row","col")), out_specs=(P(),P(None,"col"),P("row","col")), check_vma=False)
```

```python
import jax
import jax.numpy as jnp
from jax import lax
from jax.experimental import pallas as pl
from jax.experimental.pallas import tpu as pltpu
from jax.sharding import PartitionSpec as P

MESH = pl.DeviceIdType.MESH
K = 4096
H = K // 2
S1P, S1M, F1P, F1M = 0, 1, 2, 3
S2P, S2M, F2P, F2M = 4, 9, 14, 18
NMSG = 22

class Half:
    def __init__(self, half, panel, g, ssem, rsem, x, y):
        self.h, self.panel, self.g, self.ss, self.rs = half, panel, g, ssem, rsem
        self.p, self.q = (x, y) if half == 0 else (y, x)
        w = lambda v: lax.rem(v, 4)
        self.P = [self.p, w(self.p + 3), w(self.p + 1), w(self.p + 2)]
        self.Q = [self.q, w(self.q + 3), w(self.q + 1), w(self.q + 2)]
        self.pending = []
    def col(self, p, q):
        return p * 4 + q if self.h == 0 else q * 4 + p
    def slc(self, p, q, lo, n):
        r = pl.multiple_of(self.col(p, q) * 16 + 8 * self.h, 8)
        return self.g.at[pl.ds(r, 8), pl.ds(lo, n)]
    def send(self, m, p, q, lo, n, axis, sign, own=False):
        dst = self.slc(p, q, lo, n)
        src = self.panel.at[pl.ds(8 * self.h, 8), pl.ds(lo, n)] if own else dst
        i = 1 if sign < 0 else 2
        to = self.col(self.P[i], self.q) if axis == 1 else self.col(self.p, self.Q[i])
        c = pltpu.make_async_remote_copy(src, dst, self.ss.at[self.h, m], self.rs.at[self.h, m], device_id={"col": to}, device_id_type=MESH)
        c.start()
        self.pending.append(c)
    def recv(self, m, p, q, lo, n):
        d = self.slc(p, q, lo, n)
        pltpu.make_async_remote_copy(d, d, self.ss.at[self.h, m], self.rs.at[self.h, m], device_id={"col": self.col(self.P[1], self.q)}, device_id_type=MESH).wait_recv()
    def start_own(self):
        self.send(S1P, self.p, self.q, 0, K, 1, 1, True)
        self.send(S1M, self.p, self.q, 0, K, 1, -1, True)
    def start_own2(self):
        self.send(S2P, self.p, self.q, 0, K, 2, 1, True)
        self.send(S2M, self.p, self.q, 0, K, 2, -1, True)
    def first_p(self):
        pm = self.P[1]
        self.recv(S1P, pm, self.q, 0, K)
        self.send(F1P, pm, self.q, 0, H, 1, 1)
        self.send(S2P + 1, pm, self.q, 0, K, 2, 1)
        self.send(S2M + 1, pm, self.q, 0, K, 2, -1)
    def first_m(self):
        pp = self.P[2]
        self.recv(S1M, pp, self.q, 0, K)
        self.send(F1M, pp, self.q, H, H, 1, -1)
        self.send(S2P + 2, pp, self.q, 0, K, 2, 1)
        self.send(S2M + 2, pp, self.q, 0, K, 2, -1)
    def far(self):
        po = self.P[3]
        self.recv(F1P, po, self.q, 0, H)
        self.send(S2P + 3, po, self.q, 0, H, 2, 1)
        self.send(S2M + 3, po, self.q, 0, H, 2, -1)
        self.recv(F1M, po, self.q, H, H)
        self.send(S2P + 4, po, self.q, H, H, 2, 1)
        self.send(S2M + 4, po, self.q, H, H, 2, -1)
    def second(self, s):
        ps = self.P[s]
        if s < 3:
            self.recv(S2P + s, ps, self.Q[1], 0, K)
            self.send(F2P + s, ps, self.Q[1], 0, H, 2, 1)
            self.recv(S2M + s, ps, self.Q[2], 0, K)
            self.send(F2M + s, ps, self.Q[2], H, H, 2, -1)
        else:
            self.recv(S2P + 3, ps, self.Q[1], 0, H)
            self.send(F2P + 3, ps, self.Q[1], 0, H, 2, 1)
            self.recv(S2M + 3, ps, self.Q[2], 0, H)
            self.recv(S2P + 4, ps, self.Q[1], H, H)
            self.recv(S2M + 4, ps, self.Q[2], H, H)
            self.send(F2M + 3, ps, self.Q[2], H, H, 2, -1)
    def last(self, s):
        ps, qo = self.P[s], self.Q[3]
        self.recv(F2P + s, ps, qo, 0, H)
        self.recv(F2M + s, ps, qo, H, H)


HI = lax.Precision.HIGHEST
T = 8
N = 128

def dot(a, b, ca=1, cb=0):
    return lax.dot_general(a, b, (((ca,), (cb,)), ((), ())), precision=HI, preferred_element_type=jnp.float32)

def factor_half(tiles):
    n = len(tiles)
    sub = lax.broadcasted_iota(jnp.int32, (T, N), 0)
    lane = lax.broadcasted_iota(jnp.int32, (T, N), 1)
    bl = lambda x, c: jnp.broadcast_to(x[:, c:c + 1], (T, N))
    bs = lambda x, r: jnp.broadcast_to(x[r:r + 1, :], (T, N))
    tiles = list(tiles)
    Rs, Ls = [], []
    for k in range(n):
        t = tiles[k]
        inb = (lane >= T * k) & (lane < T * k + T)
        eye = jnp.where(lane - T * k == sub, 1.0, 0.0)
        cols = [bl(t, T * k + m) for m in range(T)]
        z = jnp.where(inb, eye, t)
        u = t
        li = z
        dinv = jnp.zeros((T, N), jnp.float32)
        drs = jnp.zeros((T, N), jnp.float32)
        for j in range(T):
            piv = bs(cols[j], j)
            r = 1.0 / piv
            f = jnp.where(sub == j, 0.0, cols[j] * r)
            fl = jnp.where(sub > j, f, 0.0)
            for m in range(j + 1, T):
                cols[m] = cols[m] - f * bs(cols[m], j)
            dinv = jnp.where(sub == j, r, dinv)
            drs = jnp.where(sub == j, lax.rsqrt(piv), drs)
            z = z - f * bs(z, j)
            u = u - fl * bs(u, j)
            li = li - fl * bs(li, j)
        z = z * dinv
        row = sub + T * k
        Rs.append(jnp.where(lane >= row, u * drs, 0.0))
        Ls.append(jnp.where(lane <= row, li * drs, 0.0))
        zr = [bs(z, m) for m in range(T)]
        for i in range(k + 1, n):
            ti = tiles[i]
            c = [bl(ti, T * k + m) for m in range(T)]
            p = [c[m] * zr[m] for m in range(T)]
            while len(p) > 1:
                p = [p[a] + p[a + 1] for a in range(0, len(p), 2)]
            tiles[i] = jnp.where(inb, 0.0, ti) - p[0]
    return Rs, Ls


NC = 16
F32 = jnp.float32
BF = jnp.bfloat16
FULL = "agpc"

def make_kernel(NR, parts=FULL):
    NZ = NR // 2
    WITH_A, WITH_G, WITH_P, WITH_C = (k in parts for k in "agpc")
    def kernel(panel, trail, g_out, psum, r_out, li_out,
               g, ssem, rsem, lsem, xb, tr, t2, gp3, gx, rs16, zb, gall, pp, px, prs, pall, qs, qr):
        c = lax.axis_index("col")
        w = lax.axis_index("row")
        x, y = c // 4, lax.rem(c, 4)
        z, core = w // 2, lax.rem(w, 2)
        sib = {"row": z * 2 + 1 - core}
        cols = [lax.rem(c + i, NC) for i in range(1, NC)]
        zs = [lax.rem(z + i, NZ) for i in range(1, NZ)]
        own = pltpu.make_async_copy(panel, g.at[pl.ds(pl.multiple_of(c * 16, 16), 16), :], lsem.at[0])
        own.start()
        mine = pltpu.make_async_copy(panel.at[:, pl.ds(pl.multiple_of(c * 256, 256), 256)], xb.at[pl.ds(pl.multiple_of(c * 16, 16), 16), :], lsem.at[1])
        mine.start()
        tcopy = pltpu.make_async_copy(trail, tr, lsem.at[2])
        tcopy.start()
        A = Half(0, panel, g, ssem, rsem, x, y)
        B = Half(1, panel, g, ssem, rsem, x, y)
        bar = pltpu.get_barrier_semaphore()
        for i in range(1, NR):
            pl.semaphore_signal(bar, inc=1, device_id={"row": lax.rem(w + i, NR)}, device_id_type=MESH)
        for j in cols:
            pl.semaphore_signal(bar, inc=1, device_id={"col": j}, device_id_type=MESH)
        pl.semaphore_wait(bar, NC + NR - 2)

        def send(k, src, dst, dev):
            pltpu.make_async_remote_copy(src, dst, qs.at[k], qr.at[k], device_id=dev, device_id_type=MESH).start()
        def got(k, ref, sent=False):
            d = pltpu.make_async_remote_copy(ref, ref, qs.at[k], qr.at[k], device_id=sib, device_id_type=MESH)
            d.wait_send() if sent else d.wait_recv()

        def g_rows():
            for j in cols:
                send(0, panel.at[:, pl.ds(pl.multiple_of(j * 256, 256), 256)], xb.at[pl.ds(pl.multiple_of(c * 16, 16), 16), :], {"col": j})
        def g_local():
            mine.wait()
            got(0, xb.at[pl.ds(0, 240), :])
            hi = xb[:128, :]
            xv = xb[...]
            top = dot(hi, xv, 1, 1)
            low = dot(xb[128:, :], xb[128:, :], 1, 1)
            gp3[pl.ds(0, 128), 0, :] = top[:, :128]
            gp3[pl.ds(128, 128), 0, :] = top[:, 128:]
            gp3[pl.ds(256, 128), 0, :] = low
            send(1, gp3.at[pl.ds((1 - core) * 192, 192)], gx, sib)
        def g_pair():
            got(1, gx)
            gx[...] += gp3[pl.ds(core * 192, 192)]
            for i, j in enumerate(cols):
                send(2, gx.at[pl.ds(j * 12, 12)], rs16.at[pl.ds(i * 12, 12)], {"col": j})
        def g_plane():
            got(2, rs16)
            acc = gx[pl.ds(c * 12, 12)]
            for i in range(NC - 1):
                acc = acc + rs16[pl.ds(i * 12, 12)]
            zb[pl.ds(z * 12, 12)] = acc
            for j in zs:
                send(3, zb.at[pl.ds(z * 12, 12)], zb.at[pl.ds(z * 12, 12)], {"row": j * 2 + core})
        def g_all():
            got(3, zb.at[pl.ds(0, 12 * (NZ - 1))])
            acc = zb[pl.ds(0, 12)]
            for i in range(1, NZ):
                acc = acc + zb[pl.ds(i * 12, 12)]
            at = pl.ds(core * 192 + c * 12, 12)
            gall[at] = acc
            for j in cols:
                send(4, gall.at[at], gall.at[at], {"col": j})
        def g_cols():
            got(4, gall.at[pl.ds(0, 180)])
            at = pl.ds(core * 192, 192)
            send(5, gall.at[at], gall.at[at], sib)
        def g_done():
            got(5, gall.at[pl.ds(0, 192)])

        def rows_of(s):
            a = [16 * A.col(A.P[s], q) for q in range(4)]
            b = [16 * B.col(B.P[s], q) + 8 for q in range(4)]
            return [pl.multiple_of(v, 8) for v in a + b]
        CH = 512
        def p_local(lo, n):
            rows = [r for s in range(lo, lo + n) for r in rows_of(s)]
            m = 64 * n
            def step(i, acc):
                k0 = pl.multiple_of(i * CH, CH)
                v = jnp.concatenate([g[pl.ds(r, 8), pl.ds(k0, CH)] for r in rows], axis=0)
                hi = v.astype(BF)
                l = (v - hi.astype(F32)).astype(BF)
                return acc + jnp.dot(jnp.concatenate([hi, l], axis=0), t2[pl.ds(k0, CH), :], preferred_element_type=F32)
            acc = lax.fori_loop(0, K // CH, step, jnp.zeros((2 * m, 256), F32))
            v = (acc[:m, 128:] + acc[m:, 128:]) + acc[m:, :128] + acc[:m, :128]
            pp[pl.ds(64 * lo, m), 0, :] = v
        def p_pair(k, lo, n):
            h = 32 * n
            send(k, pp.at[pl.ds(64 * lo + (1 - core) * h, h)], px.at[pl.ds(32 * lo, h)], sib)
        def p_scatter(k, lo, n):
            h = 32 * n; u = h // NZ
            got(k, px.at[pl.ds(0, h)])
            at = pl.ds(32 * lo, h)
            px[at] += pp[pl.ds(64 * lo + core * h, h)]
            for i, j in enumerate(zs):
                send(k + 1, px.at[pl.ds(32 * lo + j * u, u)], prs.at[pl.ds((NZ - 1) * (32 // NZ) * lo + i * u, u)], {"row": j * 2 + core})
        def p_spread(k, lo, n):
            h = 32 * n; u = h // NZ
            got(k + 1, prs.at[pl.ds(0, (NZ - 1) * u)])
            acc = px[pl.ds(32 * lo + z * u, u)]
            for i in range(NZ - 1):
                acc = acc + prs[pl.ds((NZ - 1) * (32 // NZ) * lo + i * u, u)]
            at = pl.ds(64 * lo + core * h + z * u, u)
            pall[at] = acc
            for j in zs:
                send(k + 2, pall.at[at], pall.at[at], {"row": j * 2 + core})
        def p_back(k, lo, n):
            h = 32 * n; u = h // NZ
            got(k + 2, pall.at[pl.ds(0, (NZ - 1) * u)])
            at = pl.ds(64 * lo + core * h, h)
            send(k + 3, pall.at[at], pall.at[at], sib)
        def p_done(k, lo, n):
            got(k + 3, pall.at[pl.ds(0, 32 * n)])
            for s in range(lo, lo + n):
                for t, r in enumerate(rows_of(s)):
                    psum[pl.ds(r, 8), :] = pall[pl.ds(64 * s + 8 * t, 8), 0, :]
        def p_sent(k, n):
            h = 32 * n; u = h // NZ
            got(k, px.at[pl.ds(0, h)], True)
            got(k + 1, prs.at[pl.ds(0, (NZ - 1) * u)], True)
            got(k + 2, pall.at[pl.ds(0, (NZ - 1) * u)], True)
            got(k + 3, pall.at[pl.ds(0, h)], True)

        def f_half(read, o):
            R, L = factor_half([read(i) for i in range(16)])
            for i in range(16):
                r_out[o + 8 * i:o + 8 * i + 8, o:o + 128] = R[i]
                li_out[o + 8 * i:o + 8 * i + 8, o:o + 128] = L[i]
        def f_first():
            f_half(lambda i: gall[pl.ds(8 * i, 8), 0, :], 0)
        def f_second():
            linv1 = li_out[:128, :128]
            r12 = dot(linv1, gall[pl.ds(128, 128), 0, :])
            r_out[:128, 128:] = r12
            r_out[128:, :128] = jnp.zeros((128, 128), F32)
            li_out[:128, 128:] = jnp.zeros((128, 128), F32)
            s = gall[pl.ds(256, 128), 0, :] - dot(r12, r12, 0, 0)
            f_half(lambda i: s[8 * i:8 * i + 8, :], 128)
            li_out[128:, :128] = -dot(li_out[128:, 128:], dot(r12, linv1, 0, 0))
        def split_trail():
            tcopy.wait()
            @pl.loop(0, K // CH)
            def _(i):
                at = pl.ds(pl.multiple_of(i * CH, CH), CH)
                v = tr[at, :]
                hi = v.astype(BF)
                t2[at, :128] = hi
                t2[at, 128:] = (v - hi.astype(F32)).astype(BF)

        def G(f, *a):
            if WITH_G: f(*a)
        def GA(*names):
            if WITH_A:
                for nm in names:
                    nm, *a = nm if isinstance(nm, tuple) else (nm,)
                    getattr(A, nm)(*a); getattr(B, nm)(*a)
        def PR(f, *a):
            if WITH_P: f(*a)
        G(g_rows)
        GA("start_own")
        split_trail()
        G(g_local)
        G(g_pair)
        GA("start_own2", "first_p", "first_m")
        G(g_plane)
        GA(("second", 0), "far", ("second", 1), ("second", 2))
        G(g_all)
        GA(("second", 3), ("last", 0), ("last", 1), ("last", 2))
        own.wait()
        PR(p_local, 0, 3)
        PR(p_pair, 6, 0, 3)
        G(g_cols)
        PR(p_scatter, 6, 0, 3)
        G(g_done)
        GA(("last", 3))
        gcopy = pltpu.make_async_copy(g, g_out, lsem.at[3])
        gcopy.start()
        PR(p_local, 3, 1)
        PR(p_pair, 10, 3, 1)
        if WITH_C: f_first()
        PR(p_spread, 6, 0, 3)
        PR(p_scatter, 10, 3, 1)
        if WITH_C: f_second()
        PR(p_back, 6, 0, 3)
        PR(p_spread, 10, 3, 1)
        PR(p_done, 6, 0, 3)
        PR(p_back, 10, 3, 1)
        PR(p_done, 10, 3, 1)
        gcopy.wait()
        if not WITH_G:
            mine.wait()
        for q in A.pending + B.pending:
            q.wait_send()
        if WITH_G:
            got(0, xb.at[pl.ds(0, 240), :], True)
            got(1, gx, True)
            got(2, rs16, True)
            got(3, zb.at[pl.ds(0, 12 * (NZ - 1))], True)
            got(4, gall.at[pl.ds(0, 180)], True)
            got(5, gall.at[pl.ds(0, 192)], True)
        PR(p_sent, 6, 3)
        PR(p_sent, 10, 1)
    V = pl.BlockSpec(memory_space=pltpu.VMEM)
    HB = pl.BlockSpec(memory_space=pltpu.HBM)
    def call(panel, trail):
        sh = lambda *s: jax.ShapeDtypeStruct(s, F32)
        vm = lambda *s: pltpu.VMEM(s, F32)
        return pl.pallas_call(kernel,
            out_shape=[sh(256, K), sh(256, 128), sh(256, 256), sh(256, 256)],
            in_specs=[HB, HB], out_specs=[HB, V, V, V],
            scratch_shapes=[vm(256, K), pltpu.SemaphoreType.DMA((2, NMSG)), pltpu.SemaphoreType.DMA((2, NMSG)), pltpu.SemaphoreType.DMA((4,)),
                vm(256, 256), vm(K, 128), pltpu.VMEM((K, 256), BF),
                vm(384, 1, 128), vm(192, 1, 128), vm(180, 1, 128), vm(12 * NZ, 1, 128), vm(384, 1, 128),
                vm(256, 1, 128), vm(128, 1, 128), vm(128 * (NZ - 1) // NZ, 1, 128), vm(256, 1, 128),
                pltpu.SemaphoreType.DMA((14,)), pltpu.SemaphoreType.DMA((14,))],
            compiler_params=pltpu.CompilerParams(collective_id=0, has_side_effects=True, vmem_limit_bytes=60 << 20))(panel, trail)
    return call

UC = 512
F32 = jnp.float32
def finish(psum, r_in, li, g, trail, r_out, top, out, cf):
    @pl.when(pl.program_id(0) == 0)
    def _():
        r_out[...] = r_in[...]
        t = dot(li[...], psum[...])
        top[...] = t
        cf[...] = dot(li[...], t, 0, 0)
    out[...] = trail[...] - dot(g[...], cf[...], 0, 0)

def finish_call(psum, r_in, li, g, trail):
    V = pl.BlockSpec(memory_space=pltpu.VMEM)
    W = lambda s: pl.BlockSpec(s, lambda i: (0, 0))
    sh = lambda *s: jax.ShapeDtypeStruct(s, F32)
    return pl.pallas_call(finish, grid=(K // UC,),
        in_specs=[W((256, 128)), W((256, 256)), W((256, 256)), pl.BlockSpec((256, UC), lambda i: (0, i)), pl.BlockSpec((UC, 128), lambda i: (i, 0))],
        out_specs=[W((256, 256)), W((256, 128)), pl.BlockSpec((UC, 128), lambda i: (i, 0))],
        out_shape=[sh(256, 256), sh(256, 128), sh(K, 128)],
        scratch_shapes=[pltpu.VMEM((256, 128), F32)],
        compiler_params=pltpu.CompilerParams(vmem_limit_bytes=60 << 20))(psum, r_in, li, g, trail)

def solution(mesh):
    k=make_kernel(mesh.shape["row"])
    def body(panel, trail):
        g, ps, r, li = k(panel, trail)
        return tuple(finish_call(ps, r, li, g, trail))
    return jax.shard_map(body, mesh=mesh, in_specs=(P("col","row"),P("row","col")), out_specs=(P(),P(None,"col"),P("row","col")), check_vma=False)
```

```python
import jax
import jax.numpy as jnp
from jax import lax
from jax.experimental import pallas as pl
from jax.experimental.pallas import tpu as pltpu
from jax.sharding import PartitionSpec as P

MESH = pl.DeviceIdType.MESH
K = 4096
H = K // 2
S1P, S1M, F1P, F1M = 0, 1, 2, 3
S2P, S2M, F2P, F2M = 4, 9, 14, 18
NMSG = 22

class Half:
    def __init__(self, half, panel, g, ssem, rsem, x, y):
        self.h, self.panel, self.g, self.ss, self.rs = half, panel, g, ssem, rsem
        self.p, self.q = (x, y) if half == 0 else (y, x)
        w = lambda v: lax.rem(v, 4)
        self.P = [self.p, w(self.p + 3), w(self.p + 1), w(self.p + 2)]
        self.Q = [self.q, w(self.q + 3), w(self.q + 1), w(self.q + 2)]
        self.pending = []
    def col(self, p, q):
        return p * 4 + q if self.h == 0 else q * 4 + p
    def slc(self, p, q, lo, n):
        r = pl.multiple_of(self.col(p, q) * 16 + 8 * self.h, 8)
        return self.g.at[pl.ds(r, 8), pl.ds(lo, n)]
    def send(self, m, p, q, lo, n, axis, sign, own=False):
        dst = self.slc(p, q, lo, n)
        src = self.panel.at[pl.ds(8 * self.h, 8), pl.ds(lo, n)] if own else dst
        i = 1 if sign < 0 else 2
        to = self.col(self.P[i], self.q) if axis == 1 else self.col(self.p, self.Q[i])
        c = pltpu.make_async_remote_copy(src, dst, self.ss.at[self.h, m], self.rs.at[self.h, m], device_id={"col": to}, device_id_type=MESH)
        c.start()
        self.pending.append(c)
    def recv(self, m, p, q, lo, n):
        d = self.slc(p, q, lo, n)
        pltpu.make_async_remote_copy(d, d, self.ss.at[self.h, m], self.rs.at[self.h, m], device_id={"col": self.col(self.P[1], self.q)}, device_id_type=MESH).wait_recv()
    def start_own(self):
        self.send(S1P, self.p, self.q, 0, K, 1, 1, True)
        self.send(S1M, self.p, self.q, 0, K, 1, -1, True)
    def start_own2(self):
        self.send(S2P, self.p, self.q, 0, K, 2, 1, True)
        self.send(S2M, self.p, self.q, 0, K, 2, -1, True)
    def first_p(self):
        pm = self.P[1]
        self.recv(S1P, pm, self.q, 0, K)
        self.send(F1P, pm, self.q, 0, H, 1, 1)
        self.send(S2P + 1, pm, self.q, 0, K, 2, 1)
        self.send(S2M + 1, pm, self.q, 0, K, 2, -1)
    def first_m(self):
        pp = self.P[2]
        self.recv(S1M, pp, self.q, 0, K)
        self.send(F1M, pp, self.q, H, H, 1, -1)
        self.send(S2P + 2, pp, self.q, 0, K, 2, 1)
        self.send(S2M + 2, pp, self.q, 0, K, 2, -1)
    def far(self):
        po = self.P[3]
        self.recv(F1P, po, self.q, 0, H)
        self.send(S2P + 3, po, self.q, 0, H, 2, 1)
        self.send(S2M + 3, po, self.q, 0, H, 2, -1)
        self.recv(F1M, po, self.q, H, H)
        self.send(S2P + 4, po, self.q, H, H, 2, 1)
        self.send(S2M + 4, po, self.q, H, H, 2, -1)
    def second(self, s):
        ps = self.P[s]
        if s < 3:
            self.recv(S2P + s, ps, self.Q[1], 0, K)
            self.send(F2P + s, ps, self.Q[1], 0, H, 2, 1)
            self.recv(S2M + s, ps, self.Q[2], 0, K)
            self.send(F2M + s, ps, self.Q[2], H, H, 2, -1)
        else:
            self.recv(S2P + 3, ps, self.Q[1], 0, H)
            self.send(F2P + 3, ps, self.Q[1], 0, H, 2, 1)
            self.recv(S2M + 3, ps, self.Q[2], 0, H)
            self.recv(S2P + 4, ps, self.Q[1], H, H)
            self.recv(S2M + 4, ps, self.Q[2], H, H)
            self.send(F2M + 3, ps, self.Q[2], H, H, 2, -1)
    def last(self, s):
        ps, qo = self.P[s], self.Q[3]
        self.recv(F2P + s, ps, qo, 0, H)
        self.recv(F2M + s, ps, qo, H, H)


HI = lax.Precision.HIGHEST
T = 8
N = 128

def dot(a, b, ca=1, cb=0):
    return lax.dot_general(a, b, (((ca,), (cb,)), ((), ())), precision=HI, preferred_element_type=jnp.float32)

def factor_steps(tiles, put):
    n = len(tiles)
    sub = lax.broadcasted_iota(jnp.int32, (T, N), 0)
    lane = lax.broadcasted_iota(jnp.int32, (T, N), 1)
    bl = lambda x, c: jnp.broadcast_to(x[:, c:c + 1], (T, N))
    bs = lambda x, r: jnp.broadcast_to(x[r:r + 1, :], (T, N))
    tiles = list(tiles)
    for k in range(n):
        t = tiles[k]
        inb = (lane >= T * k) & (lane < T * k + T)
        eye = jnp.where(lane - T * k == sub, 1.0, 0.0)
        cols = [bl(t, T * k + m) for m in range(T)]
        z = jnp.where(inb, eye, t)
        u = t
        li = z
        dinv = jnp.zeros((T, N), jnp.float32)
        drs = jnp.zeros((T, N), jnp.float32)
        for j in range(T):
            piv = bs(cols[j], j)
            r = 1.0 / piv
            f = jnp.where(sub == j, 0.0, cols[j] * r)
            fl = jnp.where(sub > j, f, 0.0)
            for m in range(j + 1, T):
                cols[m] = cols[m] - f * bs(cols[m], j)
            dinv = jnp.where(sub == j, r, dinv)
            drs = jnp.where(sub == j, lax.rsqrt(piv), drs)
            z = z - f * bs(z, j)
            u = u - fl * bs(u, j)
            li = li - fl * bs(li, j)
        z = z * dinv
        row = sub + T * k
        put(k, jnp.where(lane >= row, u * drs, 0.0), jnp.where(lane <= row, li * drs, 0.0))
        zr = [bs(z, m) for m in range(T)]
        for i in range(k + 1, n):
            ti = tiles[i]
            c = [bl(ti, T * k + m) for m in range(T)]
            p = [c[m] * zr[m] for m in range(T)]
            while len(p) > 1:
                p = [p[a] + p[a + 1] for a in range(0, len(p), 2)]
            tiles[i] = jnp.where(inb, 0.0, ti) - p[0]
        yield k


NC = 16
F32 = jnp.float32
BF = jnp.bfloat16
ORDER = ("gr own sp gl",
         "gp own2 fp fm",
         "gpl s0 far s1",
         "s2 s3 ga l0",
         "l1 l2 ow p1",
         "sc1 l3 p2 gc",
         "sc2 gd f sp1",
         "f f sp2 f",
         "f bk1 f f",
         "f bk2 e1 e2",
         "up")
CUT = 192
LIMIT = 60 << 20

def split(v):
    hi = v.astype(BF)
    return hi, (v - hi.astype(F32)).astype(BF)

def make_kernel(NR, order=ORDER):
    NZ = NR // 2
    def kernel(panel, trail, r_out, top_out, upd,
               g, li, ssem, rsem, lsem, us, xb, tr, t2, gp3, gx, rs16, zb, gall, pp, px, prs, pall, pn, qs, qr):
        c = lax.axis_index("col")
        w = lax.axis_index("row")
        x, y = c // 4, lax.rem(c, 4)
        z, core = w // 2, lax.rem(w, 2)
        sib = {"row": z * 2 + 1 - core}
        cols = [lax.rem(c + i, NC) for i in range(1, NC)]
        zs = [lax.rem(z + i, NZ) for i in range(1, NZ)]
        own = pltpu.make_async_copy(panel, g.at[pl.ds(pl.multiple_of(c * 16, 16), 16), :], lsem.at[0])
        own.start()
        mine = pltpu.make_async_copy(panel.at[:, pl.ds(pl.multiple_of(c * 256, 256), 256)], xb.at[pl.ds(pl.multiple_of(c * 16, 16), 16), :], lsem.at[1])
        mine.start()
        tcopy = pltpu.make_async_copy(trail, tr, lsem.at[2])
        tcopy.start()
        A = Half(0, panel, g, ssem, rsem, x, y)
        B = Half(1, panel, g, ssem, rsem, x, y)
        bar = pltpu.get_barrier_semaphore()
        for i in range(1, NR):
            pl.semaphore_signal(bar, inc=1, device_id={"row": lax.rem(w + i, NR)}, device_id_type=MESH)
        for j in cols:
            pl.semaphore_signal(bar, inc=1, device_id={"col": j}, device_id_type=MESH)
        pl.semaphore_wait(bar, NC + NR - 2)

        def send(k, src, dst, dev):
            pltpu.make_async_remote_copy(src, dst, qs.at[k], qr.at[k], device_id=dev, device_id_type=MESH).start()
        def got(k, ref, sent=False):
            d = pltpu.make_async_remote_copy(ref, ref, qs.at[k], qr.at[k], device_id=sib, device_id_type=MESH)
            d.wait_send() if sent else d.wait_recv()

        def g_rows():
            for j in cols:
                send(0, panel.at[:, pl.ds(pl.multiple_of(j * 256, 256), 256)], xb.at[pl.ds(pl.multiple_of(c * 16, 16), 16), :], {"col": j})
        def g_local():
            mine.wait()
            got(0, xb.at[pl.ds(0, 240), :])
            hi = xb[:128, :]
            xv = xb[...]
            top = dot(hi, xv, 1, 1)
            low = dot(xb[128:, :], xb[128:, :], 1, 1)
            gp3[pl.ds(0, 128), 0, :] = top[:, :128]
            gp3[pl.ds(128, 128), 0, :] = top[:, 128:]
            gp3[pl.ds(256, 128), 0, :] = low
            send(1, gp3.at[pl.ds((1 - core) * 192, 192)], gx, sib)
        def g_pair():
            got(1, gx)
            gx[...] += gp3[pl.ds(core * 192, 192)]
            for i, j in enumerate(cols):
                send(2, gx.at[pl.ds(j * 12, 12)], rs16.at[pl.ds(i * 12, 12)], {"col": j})
        def g_plane():
            got(2, rs16)
            acc = gx[pl.ds(c * 12, 12)]
            for i in range(NC - 1):
                acc = acc + rs16[pl.ds(i * 12, 12)]
            zb[pl.ds(z * 12, 12)] = acc
            for j in zs:
                send(3, zb.at[pl.ds(z * 12, 12)], zb.at[pl.ds(z * 12, 12)], {"row": j * 2 + core})
        def g_all():
            got(3, zb.at[pl.ds(0, 12 * (NZ - 1))])
            acc = zb[pl.ds(0, 12)]
            for i in range(1, NZ):
                acc = acc + zb[pl.ds(i * 12, 12)]
            at = pl.ds(core * 192 + c * 12, 12)
            gall[at] = acc
            for j in cols:
                send(4, gall.at[at], gall.at[at], {"col": j})
        def g_cols():
            got(4, gall.at[pl.ds(0, 180)])
            at = pl.ds(core * 192, 192)
            send(5, gall.at[at], gall.at[at], sib)
        def g_done():
            got(5, gall.at[pl.ds(0, 192)])

        tiles = [(hf, t, q) for t in range(4) for hf in (A, B) for q in range(4)]
        rows = [pl.multiple_of(16 * hf.col(hf.P[t], hf.Q[q]) + 8 * hf.h, 8) for hf, t, q in tiles]
        base = (0, CUT, 256)
        CH = 512
        def p_local(i):
            lo, hi_ = base[i], base[i + 1]
            m = hi_ - lo
            mine_ = rows[lo // 8:hi_ // 8]
            def step(n, acc):
                k0 = pl.multiple_of(n * CH, CH)
                v = jnp.concatenate([g[pl.ds(r, 8), pl.ds(k0, CH)] for r in mine_], axis=0)
                hi, l = split(v)
                return acc + jnp.dot(jnp.concatenate([hi, l], axis=0), t2[pl.ds(k0, CH), :], preferred_element_type=F32)
            acc = lax.fori_loop(0, K // CH, step, jnp.zeros((2 * m, 256), F32))
            pp[pl.ds(lo, m), 0, :] = ((acc[m:, 128:] + acc[:m, 128:]) + acc[m:, :128]) + acc[:m, :128]
            h = m // 2
            send(6 + 4 * i, pp.at[pl.ds(lo + (1 - core) * h, h)], px.at[pl.ds(lo // 2, h)], sib)
        def p_pair(i):
            lo, h = base[i], (base[i + 1] - base[i]) // 2
            at = pl.ds(lo // 2, h)
            got(6 + 4 * i, px.at[at])
            return at, px[at] + pp[pl.ds(lo + core * h, h)]
        def sizes(i):
            h = (base[i + 1] - base[i]) // 2
            u = h // NZ
            return base[i], h, u, (NZ - 1) * base[i] // (2 * NZ)
        def p_scatter(i):
            lo, h, u, o = sizes(i)
            at, v = p_pair(i)
            px[at] = v
            for n, j in enumerate(zs):
                send(7 + 4 * i, px.at[pl.ds(lo // 2 + j * u, u)], prs.at[pl.ds(o + n * u, u)], {"row": j * 2 + core})
        def p_spread(i):
            lo, h, u, o = sizes(i)
            got(7 + 4 * i, prs.at[pl.ds(o, (NZ - 1) * u)])
            acc = px[pl.ds(lo // 2 + z * u, u)]
            for n in range(NZ - 1):
                acc = acc + prs[pl.ds(o + n * u, u)]
            at = pl.ds(lo + core * h + z * u, u)
            pall[at] = acc
            for j in zs:
                send(8 + 4 * i, pall.at[at], pall.at[at], {"row": j * 2 + core})
        def p_back(i):
            lo, h, u, o = sizes(i)
            got(8 + 4 * i, pall.at[pl.ds(0, (NZ - 1) * u)])
            at = pl.ds(lo + core * h, h)
            send(9 + 4 * i, pall.at[at], pall.at[at], sib)
        def p_end(i):
            lo, h, u, o = sizes(i)
            got(9 + 4 * i, pall.at[pl.ds(0, h)])
            for t in range(h // 4):
                pn[pl.ds(rows[lo // 8 + t], 8), :] = pall[pl.ds(lo + 8 * t, 8), 0, :]
        def p_sent():
            for i in range(2):
                lo, h, u, o = sizes(i)
                got(6 + 4 * i, px.at[pl.ds(0, h)], True)
                got(7 + 4 * i, prs.at[pl.ds(0, (NZ - 1) * u)], True)
                got(8 + 4 * i, pall.at[pl.ds(0, (NZ - 1) * u)], True)
                got(9 + 4 * i, pall.at[pl.ds(0, h)], True)

        def put_at(o):
            def put(k, rt, lt):
                r_out[o + 8 * k:o + 8 * k + 8, o:o + 128] = rt
                li[o + 8 * k:o + 8 * k + 8, o:o + 128] = lt
            return put
        def factor():
            for k in factor_steps([gall[pl.ds(8 * i, 8), 0, :] for i in range(16)], put_at(0)):
                if k % 4 == 3: yield
            linv1 = li[:128, :128]
            r12 = dot(linv1, gall[pl.ds(128, 128), 0, :])
            r_out[:128, 128:] = r12
            r_out[128:, :128] = jnp.zeros((128, 128), F32)
            li[:128, 128:] = jnp.zeros((128, 128), F32)
            s = gall[pl.ds(256, 128), 0, :] - dot(r12, r12, 0, 0)
            for k in factor_steps([s[8 * i:8 * i + 8, :] for i in range(16)], put_at(128)):
                if k == 15:
                    li[128:, :128] = -dot(li[128:, 128:], dot(r12, linv1, 0, 0))
                    xb[...] = dot(li[...], li[...], 0, 0)
                if k % 4 == 3: yield
        steps = factor()
        def update():
            p = pn[...]
            hi, lo = split(dot(p, xb[...], 0, 0))
            cf = jnp.concatenate([hi, lo], axis=0)
            top_out[...] = dot(li[...], p)
            for n in range(K // CH):
                at = pl.ds(n * CH, CH)
                hi, lo = split(g[:, at])
                a = jnp.dot(cf, hi, preferred_element_type=F32)
                b = jnp.dot(cf, lo, preferred_element_type=F32)
                v = ((b[128:] + a[128:]) + b[:128]) + a[:128]
                tr[at, :] -= v.T
                pltpu.make_async_copy(tr.at[at, :], upd.at[at, :], us.at[n]).start()
            for n in range(K // CH):
                at = pl.ds(n * CH, CH)
                pltpu.make_async_copy(tr.at[at, :], upd.at[at, :], us.at[n]).wait()
        def split_trail():
            tcopy.wait()
            @pl.loop(0, K // CH)
            def _(i):
                at = pl.ds(pl.multiple_of(i * CH, CH), CH)
                hi, lo = split(tr[at, :])
                t2[at, :128] = hi
                t2[at, 128:] = lo

        def both(name, *a):
            for hf in (A, B):
                getattr(hf, name)(*a)
        def adv(n):
            for _ in range(n): next(steps, None)
        do = {"gr": g_rows, "gl": g_local, "gp": g_pair, "gpl": g_plane, "ga": g_all, "gc": g_cols, "gd": g_done, "sp": split_trail,
              "own": lambda: both("start_own"), "own2": lambda: both("start_own2"), "fp": lambda: both("first_p"), "fm": lambda: both("first_m"), "far": lambda: both("far"),
              "s0": lambda: both("second", 0), "s1": lambda: both("second", 1), "s2": lambda: both("second", 2), "s3": lambda: both("second", 3),
              "l0": lambda: both("last", 0), "l1": lambda: both("last", 1), "l2": lambda: both("last", 2), "l3": lambda: both("last", 3),
              "p1": lambda: p_local(0), "p2": lambda: p_local(1), "sc1": lambda: p_scatter(0), "sp1": lambda: p_spread(0), "bk1": lambda: p_back(0), "e1": lambda: p_end(0),
              "sc2": lambda: p_scatter(1), "sp2": lambda: p_spread(1), "bk2": lambda: p_back(1), "e2": lambda: p_end(1),
              "up": update, "ow": own.wait,
              "f": lambda: adv(1)}
        todo = [w for l in order for w in l.split()]
        for nm in todo:
            do[nm]()
        if "gl" not in todo:
            mine.wait()
        if "ow" not in todo:
            own.wait()
        if "sp" not in todo:
            tcopy.wait()
        for q in A.pending + B.pending:
            q.wait_send()
        if "gr" in todo:
            got(0, xb.at[pl.ds(0, 240), :], True)
            got(1, gx, True)
            got(2, rs16, True)
            got(3, zb.at[pl.ds(0, 12 * (NZ - 1))], True)
            got(4, gall.at[pl.ds(0, 180)], True)
            got(5, gall.at[pl.ds(0, 192)], True)
        if "p1" in todo:
            p_sent()
    V = pl.BlockSpec(memory_space=pltpu.VMEM)
    HB = pl.BlockSpec(memory_space=pltpu.HBM)
    def call(panel, trail):
        sh = lambda *s: jax.ShapeDtypeStruct(s, F32)
        vm = lambda *s: pltpu.VMEM(s, F32)
        return pl.pallas_call(kernel,
            out_shape=[sh(256, 256), sh(256, 128), sh(K, 128)],
            in_specs=[HB, HB], out_specs=[V, V, HB],
            scratch_shapes=[vm(256, K), vm(256, 256), pltpu.SemaphoreType.DMA((2, NMSG)), pltpu.SemaphoreType.DMA((2, NMSG)), pltpu.SemaphoreType.DMA((3,)), pltpu.SemaphoreType.DMA((8,)),
                vm(256, 256), vm(K, 128), pltpu.VMEM((K, 256), BF),
                vm(384, 1, 128), vm(192, 1, 128), vm(180, 1, 128), vm(12 * NZ, 1, 128), vm(384, 1, 128),
                vm(256, 1, 128), vm(128, 1, 128), vm(128 * (NZ - 1) // NZ, 1, 128), vm(256, 1, 128), vm(256, 128),
                pltpu.SemaphoreType.DMA((14,)), pltpu.SemaphoreType.DMA((14,))],
            compiler_params=pltpu.CompilerParams(collective_id=0, has_side_effects=True, vmem_limit_bytes=LIMIT))(panel, trail)
    return call

PARTS = (1, 1, 4)
def deliver(a, b, c, a_out, b_out, c_out, a_buf, b_buf, c_buf, si, so):
    moves = []
    for src, buf, dst, parts in ((c, c_buf, c_out, PARTS[2]), (a, a_buf, a_out, PARTS[0]), (b, b_buf, b_out, PARTS[1])):
        n = src.shape[0] // parts
        for i in range(parts):
            at, k = pl.ds(i * n, n), len(moves)
            moves.append((pltpu.make_async_copy(src.at[at, :], buf.at[at, :], si.at[k]), pltpu.make_async_copy(buf.at[at, :], dst.at[at, :], so.at[k])))
    for i, _ in moves: i.start()
    for i, o in moves:
        i.wait()
        o.start()
    for _, o in moves: o.wait()

def deliver_call(*vals):
    HB = pl.BlockSpec(memory_space=pl.ANY)
    return pl.pallas_call(deliver, in_specs=[HB] * 3, out_specs=[HB] * 3,
        out_shape=[jax.ShapeDtypeStruct(v.shape, F32) for v in vals],
        scratch_shapes=[pltpu.VMEM(v.shape, F32) for v in vals] + [pltpu.SemaphoreType.DMA((sum(PARTS),))] * 2,
        compiler_params=pltpu.CompilerParams(vmem_limit_bytes=60 << 20))(*vals)

def solution(mesh):
    call = make_kernel(mesh.shape["row"])
    def body(panel, trailing):
        return tuple(deliver_call(*call(panel, trailing)))
    return jax.shard_map(body, mesh=mesh, in_specs=(P("col", "row"), P("row", "col")),
                         out_specs=(P(), P(None, "col"), P("row", "col")), check_vma=False)
```

```python
import jax
import jax.numpy as jnp
from jax import lax
from jax.experimental import pallas as pl
from jax.experimental.pallas import tpu as pltpu
from jax.sharding import PartitionSpec as P

MESH = pl.DeviceIdType.MESH
K = 4096
H = K // 2
S1P, S1M, F1P, F1M = 0, 1, 2, 3
S2P, S2M, F2P, F2M = 4, 9, 14, 18
NMSG = 22

class Half:
    def __init__(self, half, panel, g, ssem, rsem, x, y):
        self.h, self.panel, self.g, self.ss, self.rs = half, panel, g, ssem, rsem
        self.p, self.q = (x, y) if half == 0 else (y, x)
        w = lambda v: lax.rem(v, 4)
        self.P = [self.p, w(self.p + 3), w(self.p + 1), w(self.p + 2)]
        self.Q = [self.q, w(self.q + 3), w(self.q + 1), w(self.q + 2)]
        self.pending = []
    def col(self, p, q):
        return p * 4 + q if self.h == 0 else q * 4 + p
    def slc(self, p, q, lo, n):
        r = pl.multiple_of(self.col(p, q) * 16 + 8 * self.h, 8)
        return self.g.at[pl.ds(r, 8), pl.ds(lo, n)]
    def send(self, m, p, q, lo, n, axis, sign, own=False):
        dst = self.slc(p, q, lo, n)
        src = self.panel.at[pl.ds(8 * self.h, 8), pl.ds(lo, n)] if own else dst
        i = 1 if sign < 0 else 2
        to = self.col(self.P[i], self.q) if axis == 1 else self.col(self.p, self.Q[i])
        c = pltpu.make_async_remote_copy(src, dst, self.ss.at[self.h, m], self.rs.at[self.h, m], device_id={"col": to}, device_id_type=MESH)
        c.start()
        self.pending.append(c)
    def recv(self, m, p, q, lo, n):
        d = self.slc(p, q, lo, n)
        pltpu.make_async_remote_copy(d, d, self.ss.at[self.h, m], self.rs.at[self.h, m], device_id={"col": self.col(self.P[1], self.q)}, device_id_type=MESH).wait_recv()
    def start_own(self):
        self.send(S1P, self.p, self.q, 0, K, 1, 1, True)
        self.send(S1M, self.p, self.q, 0, K, 1, -1, True)
    def start_own2(self):
        self.send(S2P, self.p, self.q, 0, K, 2, 1, True)
        self.send(S2M, self.p, self.q, 0, K, 2, -1, True)
    def first_p(self):
        pm = self.P[1]
        self.recv(S1P, pm, self.q, 0, K)
        self.send(F1P, pm, self.q, 0, H, 1, 1)
        self.send(S2P + 1, pm, self.q, 0, K, 2, 1)
        self.send(S2M + 1, pm, self.q, 0, K, 2, -1)
    def first_m(self):
        pp = self.P[2]
        self.recv(S1M, pp, self.q, 0, K)
        self.send(F1M, pp, self.q, H, H, 1, -1)
        self.send(S2P + 2, pp, self.q, 0, K, 2, 1)
        self.send(S2M + 2, pp, self.q, 0, K, 2, -1)
    def far(self):
        po = self.P[3]
        self.recv(F1P, po, self.q, 0, H)
        self.send(S2P + 3, po, self.q, 0, H, 2, 1)
        self.send(S2M + 3, po, self.q, 0, H, 2, -1)
        self.recv(F1M, po, self.q, H, H)
        self.send(S2P + 4, po, self.q, H, H, 2, 1)
        self.send(S2M + 4, po, self.q, H, H, 2, -1)
    def second(self, s):
        ps = self.P[s]
        if s < 3:
            self.recv(S2P + s, ps, self.Q[1], 0, K)
            self.send(F2P + s, ps, self.Q[1], 0, H, 2, 1)
            self.recv(S2M + s, ps, self.Q[2], 0, K)
            self.send(F2M + s, ps, self.Q[2], H, H, 2, -1)
        else:
            self.recv(S2P + 3, ps, self.Q[1], 0, H)
            self.send(F2P + 3, ps, self.Q[1], 0, H, 2, 1)
            self.recv(S2M + 3, ps, self.Q[2], 0, H)
            self.recv(S2P + 4, ps, self.Q[1], H, H)
            self.recv(S2M + 4, ps, self.Q[2], H, H)
            self.send(F2M + 3, ps, self.Q[2], H, H, 2, -1)
    def last(self, s):
        ps, qo = self.P[s], self.Q[3]
        self.recv(F2P + s, ps, qo, 0, H)
        self.recv(F2M + s, ps, qo, H, H)


HI = lax.Precision.HIGHEST
T = 16
N = 128

def dot(a, b, ca=1, cb=0):
    return lax.dot_general(a, b, (((ca,), (cb,)), ((), ())), precision=HI, preferred_element_type=jnp.float32)

def factor_steps(tiles, put):
    n = len(tiles)
    sub = lax.broadcasted_iota(jnp.int32, (T, N), 0)
    lane = lax.broadcasted_iota(jnp.int32, (T, N), 1)
    bl = lambda x, c: jnp.broadcast_to(x[:, c:c + 1], (T, N))
    bs = lambda x, r: jnp.broadcast_to(x[r:r + 1, :], (T, N))
    tiles = list(tiles)
    for k in range(n):
        t = tiles[k]
        inb = (lane >= T * k) & (lane < T * k + T)
        eye = jnp.where(lane - T * k == sub, 1.0, 0.0)
        cols = [bl(t, T * k + m) for m in range(T)]
        z = jnp.where(inb, eye, t)
        u = t
        li = z
        dinv = jnp.zeros((T, N), jnp.float32)
        drs = jnp.zeros((T, N), jnp.float32)
        piv = bs(cols[0], 0)
        for j in range(T):
            r = 1.0 / piv
            cj = jnp.where(sub == j, 0.0, cols[j])
            cl = jnp.where(sub > j, cols[j], 0.0)
            nxt = None
            if j + 1 < T:
                nxt = bs(cols[j + 1], j + 1) - (bs(cols[j], j + 1) * bs(cols[j + 1], j)) * r
            for m in range(j + 1, T):
                cols[m] = cols[m] - (cj * bs(cols[m], j)) * r
            dinv = jnp.where(sub == j, r, dinv)
            drs = jnp.where(sub == j, lax.rsqrt(piv), drs)
            zj = bs(z, j)
            li = jnp.where(sub == j, zj, li)
            u = u - (cl * bs(u, j)) * r
            z = z - (cj * zj) * r
            piv = nxt
        z = z * dinv
        row = sub + T * k
        put(k, jnp.where(lane >= row, u * drs, 0.0), jnp.where(lane <= row, li * drs, 0.0))
        zr = [bs(z, m) for m in range(T)]
        if k + 1 < n:
            ti = tiles[k + 1]
            c = [bl(ti, T * k + m) for m in range(T)]
            p = [c[m] * zr[m] for m in range(T)]
            while len(p) > 1:
                p = [p[a] + p[a + 1] for a in range(0, len(p), 2)]
            tiles[k + 1] = jnp.where(inb, 0.0, ti) - p[0]
        if k + 2 < n:
            low = jnp.concatenate(tiles[k + 2:], axis=0)
            d = dot(low[:, T * k:T * k + T], z)
            for i in range(k + 2, n):
                tiles[i] = jnp.where(inb, 0.0, tiles[i]) - d[T * (i - k - 2):T * (i - k - 1)]
        yield k


NC = 16
F32 = jnp.float32
BF = jnp.bfloat16
ORDER = ("gr own own2 sp",
         "gl gp fp fm",
         "gpl s0 far s1",
         "s2 ow p1 s3",
         "ga sc1 l0 l1",
         "l2 l3 p2 gc",
         "sc2 gd f f",
         "sp1 f f sp2",
         "f f bk1 f",
         "f bk2 e1 e2",
         "up")
CUT = 160
LIMIT = 60 << 20

def split(v):
    hi = v.astype(BF)
    return hi, (v - hi.astype(F32)).astype(BF)

def make_kernel(NR, order=ORDER):
    NZ = NR // 2
    def kernel(panel, trail, r_out, top_out, upd,
               g, li, ssem, rsem, lsem, us, xb, tr, t2, gp3, gx, rs16, zb, gall, pp, px, prs, pall, pn, qs, qr):
        c = lax.axis_index("col")
        w = lax.axis_index("row")
        x, y = c // 4, lax.rem(c, 4)
        z, core = w // 2, lax.rem(w, 2)
        sib = {"row": z * 2 + 1 - core}
        far = lambda i, n: min(i, n - i)
        steps_c = sorted(((a, b) for a in range(4) for b in range(4) if a + b), key=lambda v: -far(v[0], 4) - far(v[1], 4))
        cols = [lax.rem(x + a, 4) * 4 + lax.rem(y + b, 4) for a, b in steps_c]
        zs = [lax.rem(z + i, NZ) for i in sorted(range(1, NZ), key=lambda i: -far(i, NZ))]
        own = pltpu.make_async_copy(panel, g.at[pl.ds(pl.multiple_of(c * 16, 16), 16), :], lsem.at[0])
        own.start()
        mine = pltpu.make_async_copy(panel.at[:, pl.ds(pl.multiple_of(c * 256, 256), 256)], xb.at[pl.ds(pl.multiple_of(c * 16, 16), 16), :], lsem.at[1])
        mine.start()
        tcopy = pltpu.make_async_copy(trail, tr, lsem.at[2])
        tcopy.start()
        A = Half(0, panel, g, ssem, rsem, x, y)
        B = Half(1, panel, g, ssem, rsem, x, y)
        bar = pltpu.get_barrier_semaphore()
        for j in zs:
            for k in range(2):
                pl.semaphore_signal(bar, inc=1, device_id={"row": j * 2 + k}, device_id_type=MESH)
        pl.semaphore_signal(bar, inc=1, device_id=sib, device_id_type=MESH)
        for j in cols:
            pl.semaphore_signal(bar, inc=1, device_id={"col": j}, device_id_type=MESH)
        pl.semaphore_wait(bar, NC + NR - 2)

        def send(k, src, dst, dev):
            pltpu.make_async_remote_copy(src, dst, qs.at[k], qr.at[k], device_id=dev, device_id_type=MESH).start()
        def got(k, ref, sent=False):
            d = pltpu.make_async_remote_copy(ref, ref, qs.at[k], qr.at[k], device_id=sib, device_id_type=MESH)
            d.wait_send() if sent else d.wait_recv()

        def g_rows():
            for j in cols:
                send(0, panel.at[:, pl.ds(pl.multiple_of(j * 256, 256), 256)], xb.at[pl.ds(pl.multiple_of(c * 16, 16), 16), :], {"col": j})
        def g_local():
            mine.wait()
            got(0, xb.at[pl.ds(0, 240), :])
            hi = xb[:128, :]
            xv = xb[...]
            top = dot(hi, xv, 1, 1)
            low = dot(xb[128:, :], xb[128:, :], 1, 1)
            gp3[pl.ds(0, 128), 0, :] = top[:, :128]
            gp3[pl.ds(128, 128), 0, :] = top[:, 128:]
            gp3[pl.ds(256, 128), 0, :] = low
            send(1, gp3.at[pl.ds((1 - core) * 192, 192)], gx, sib)
        def g_pair():
            got(1, gx)
            gx[...] += gp3[pl.ds(core * 192, 192)]
            for i, j in enumerate(cols):
                send(2, gx.at[pl.ds(j * 12, 12)], rs16.at[pl.ds(i * 12, 12)], {"col": j})
        def g_plane():
            got(2, rs16)
            acc = gx[pl.ds(c * 12, 12)]
            for i in range(NC - 1):
                acc = acc + rs16[pl.ds(i * 12, 12)]
            zb[pl.ds(z * 12, 12)] = acc
            for j in zs:
                send(3, zb.at[pl.ds(z * 12, 12)], zb.at[pl.ds(z * 12, 12)], {"row": j * 2 + core})
        def g_all():
            got(3, zb.at[pl.ds(0, 12 * (NZ - 1))])
            acc = zb[pl.ds(0, 12)]
            for i in range(1, NZ):
                acc = acc + zb[pl.ds(i * 12, 12)]
            at = pl.ds(core * 192 + c * 12, 12)
            gall[at] = acc
            for j in cols:
                send(4, gall.at[at], gall.at[at], {"col": j})
        def g_cols():
            got(4, gall.at[pl.ds(0, 180)])
            at = pl.ds(core * 192, 192)
            send(5, gall.at[at], gall.at[at], sib)
        def g_done():
            got(5, gall.at[pl.ds(0, 192)])

        early = [(t, q) for t in range(4) for q in range(3) if t < 3 or q == 0]
        late = [(t, q) for t in range(4) for q in range(4) if (t, q) not in early]
        tiles = [(hf, t, q) for t, q in early + late for hf in (A, B)]
        rows = [pl.multiple_of(16 * hf.col(hf.P[t], hf.Q[q]) + 8 * hf.h, 8) for hf, t, q in tiles]
        base = (0, CUT, 256)
        CH = 512
        def p_local(i):
            lo, hi_ = base[i], base[i + 1]
            m = hi_ - lo
            mine_ = rows[lo // 8:hi_ // 8]
            def step(n, acc):
                k0 = pl.multiple_of(n * CH, CH)
                v = jnp.concatenate([g[pl.ds(r, 8), pl.ds(k0, CH)] for r in mine_], axis=0)
                hi, l = split(v)
                return acc + jnp.dot(jnp.concatenate([hi, l], axis=0), t2[pl.ds(k0, CH), :], preferred_element_type=F32)
            acc = lax.fori_loop(0, K // CH, step, jnp.zeros((2 * m, 256), F32))
            pp[pl.ds(lo, m), 0, :] = ((acc[m:, 128:] + acc[:m, 128:]) + acc[m:, :128]) + acc[:m, :128]
            h = m // 2
            send(6 + 4 * i, pp.at[pl.ds(lo + (1 - core) * h, h)], px.at[pl.ds(lo // 2, h)], sib)
        def p_pair(i):
            lo, h = base[i], (base[i + 1] - base[i]) // 2
            at = pl.ds(lo // 2, h)
            got(6 + 4 * i, px.at[at])
            return at, px[at] + pp[pl.ds(lo + core * h, h)]
        def sizes(i):
            h = (base[i + 1] - base[i]) // 2
            u = h // NZ
            return base[i], h, u, (NZ - 1) * base[i] // (2 * NZ)
        def p_scatter(i):
            lo, h, u, o = sizes(i)
            at, v = p_pair(i)
            px[at] = v
            for n, j in enumerate(zs):
                send(7 + 4 * i, px.at[pl.ds(lo // 2 + j * u, u)], prs.at[pl.ds(o + n * u, u)], {"row": j * 2 + core})
        def p_spread(i):
            lo, h, u, o = sizes(i)
            got(7 + 4 * i, prs.at[pl.ds(o, (NZ - 1) * u)])
            acc = px[pl.ds(lo // 2 + z * u, u)]
            for n in range(NZ - 1):
                acc = acc + prs[pl.ds(o + n * u, u)]
            at = pl.ds(lo + core * h + z * u, u)
            pall[at] = acc
            for j in zs:
                send(8 + 4 * i, pall.at[at], pall.at[at], {"row": j * 2 + core})
        def p_back(i):
            lo, h, u, o = sizes(i)
            got(8 + 4 * i, pall.at[pl.ds(0, (NZ - 1) * u)])
            at = pl.ds(lo + core * h, h)
            send(9 + 4 * i, pall.at[at], pall.at[at], sib)
        def p_end(i):
            lo, h, u, o = sizes(i)
            got(9 + 4 * i, pall.at[pl.ds(0, h)])
            for t in range(h // 4):
                pn[pl.ds(rows[lo // 8 + t], 8), :] = pall[pl.ds(lo + 8 * t, 8), 0, :]
        def p_sent():
            for i in range(2):
                lo, h, u, o = sizes(i)
                got(6 + 4 * i, px.at[pl.ds(0, h)], True)
                got(7 + 4 * i, prs.at[pl.ds(0, (NZ - 1) * u)], True)
                got(8 + 4 * i, pall.at[pl.ds(0, (NZ - 1) * u)], True)
                got(9 + 4 * i, pall.at[pl.ds(0, h)], True)

        def put_at(o):
            def put(k, rt, lt):
                r_out[o + 16 * k:o + 16 * k + 16, o:o + 128] = rt
                li[o + 16 * k:o + 16 * k + 16, o:o + 128] = lt
            return put
        def factor():
            for k in factor_steps([gall[pl.ds(16 * i, 16), 0, :] for i in range(8)], put_at(0)):
                if k % 2 == 1: yield
            linv1 = li[:128, :128]
            r12 = dot(linv1, gall[pl.ds(128, 128), 0, :])
            r_out[:128, 128:] = r12
            r_out[128:, :128] = jnp.zeros((128, 128), F32)
            li[:128, 128:] = jnp.zeros((128, 128), F32)
            s = gall[pl.ds(256, 128), 0, :] - dot(r12, r12, 0, 0)
            for k in factor_steps([s[16 * i:16 * i + 16, :] for i in range(8)], put_at(128)):
                if k == 7:
                    li[128:, :128] = -dot(li[128:, 128:], dot(r12, linv1, 0, 0))
                    xb[...] = dot(li[...], li[...], 0, 0)
                if k % 2 == 1: yield
        steps = factor()
        def update():
            p = pn[...]
            hi, lo = split(dot(p, xb[...], 0, 0))
            cf = jnp.concatenate([hi, lo], axis=0)
            top_out[...] = dot(li[...], p)
            for n in range(K // CH):
                at = pl.ds(n * CH, CH)
                hi, lo = split(g[:, at])
                a = jnp.dot(cf, hi, preferred_element_type=F32)
                b = jnp.dot(cf, lo, preferred_element_type=F32)
                v = ((b[128:] + a[128:]) + b[:128]) + a[:128]
                tr[at, :] -= v.T
                pltpu.make_async_copy(tr.at[at, :], upd.at[at, :], us.at[n]).start()
            for n in range(K // CH):
                at = pl.ds(n * CH, CH)
                pltpu.make_async_copy(tr.at[at, :], upd.at[at, :], us.at[n]).wait()
        def split_trail():
            tcopy.wait()
            @pl.loop(0, K // CH)
            def _(i):
                at = pl.ds(pl.multiple_of(i * CH, CH), CH)
                hi, lo = split(tr[at, :])
                t2[at, :128] = hi
                t2[at, 128:] = lo

        def both(name, *a):
            for hf in (A, B):
                getattr(hf, name)(*a)
        def adv(n):
            for _ in range(n): next(steps, None)
        do = {"gr": g_rows, "gl": g_local, "gp": g_pair, "gpl": g_plane, "ga": g_all, "gc": g_cols, "gd": g_done, "sp": split_trail,
              "own": lambda: both("start_own"), "own2": lambda: both("start_own2"), "fp": lambda: both("first_p"), "fm": lambda: both("first_m"), "far": lambda: both("far"),
              "s0": lambda: both("second", 0), "s1": lambda: both("second", 1), "s2": lambda: both("second", 2), "s3": lambda: both("second", 3),
              "l0": lambda: both("last", 0), "l1": lambda: both("last", 1), "l2": lambda: both("last", 2), "l3": lambda: both("last", 3),
              "p1": lambda: p_local(0), "p2": lambda: p_local(1), "sc1": lambda: p_scatter(0), "sp1": lambda: p_spread(0), "bk1": lambda: p_back(0), "e1": lambda: p_end(0),
              "sc2": lambda: p_scatter(1), "sp2": lambda: p_spread(1), "bk2": lambda: p_back(1), "e2": lambda: p_end(1),
              "up": update, "ow": own.wait,
              "f": lambda: adv(1)}
        todo = [w for l in order for w in l.split()]
        for nm in todo:
            do[nm]()
        if "gl" not in todo:
            mine.wait()
        if "ow" not in todo:
            own.wait()
        if "sp" not in todo:
            tcopy.wait()
        for q in A.pending + B.pending:
            q.wait_send()
        if "gr" in todo:
            got(0, xb.at[pl.ds(0, 240), :], True)
            got(1, gx, True)
            got(2, rs16, True)
            got(3, zb.at[pl.ds(0, 12 * (NZ - 1))], True)
            got(4, gall.at[pl.ds(0, 180)], True)
            got(5, gall.at[pl.ds(0, 192)], True)
        if "p1" in todo:
            p_sent()
    V = pl.BlockSpec(memory_space=pltpu.VMEM)
    HB = pl.BlockSpec(memory_space=pltpu.HBM)
    def call(panel, trail):
        sh = lambda *s: jax.ShapeDtypeStruct(s, F32)
        vm = lambda *s: pltpu.VMEM(s, F32)
        return pl.pallas_call(kernel,
            out_shape=[sh(256, 256), sh(256, 128), sh(K, 128)],
            in_specs=[HB, HB], out_specs=[V, V, HB],
            scratch_shapes=[vm(256, K), vm(256, 256), pltpu.SemaphoreType.DMA((2, NMSG)), pltpu.SemaphoreType.DMA((2, NMSG)), pltpu.SemaphoreType.DMA((3,)), pltpu.SemaphoreType.DMA((8,)),
                vm(256, 256), vm(K, 128), pltpu.VMEM((K, 256), BF),
                vm(384, 1, 128), vm(192, 1, 128), vm(180, 1, 128), vm(12 * NZ, 1, 128), vm(384, 1, 128),
                vm(256, 1, 128), vm(128, 1, 128), vm(128 * (NZ - 1) // NZ, 1, 128), vm(256, 1, 128), vm(256, 128),
                pltpu.SemaphoreType.DMA((14,)), pltpu.SemaphoreType.DMA((14,))],
            compiler_params=pltpu.CompilerParams(collective_id=0, has_side_effects=True, vmem_limit_bytes=LIMIT))(panel, trail)
    return call

PARTS = (1, 1, 4)
def deliver(a, b, c, a_out, b_out, c_out, a_buf, b_buf, c_buf, si, so):
    moves = []
    for src, buf, dst, parts in ((c, c_buf, c_out, PARTS[2]), (a, a_buf, a_out, PARTS[0]), (b, b_buf, b_out, PARTS[1])):
        n = src.shape[0] // parts
        for i in range(parts):
            at, k = pl.ds(i * n, n), len(moves)
            moves.append((pltpu.make_async_copy(src.at[at, :], buf.at[at, :], si.at[k]), pltpu.make_async_copy(buf.at[at, :], dst.at[at, :], so.at[k])))
    for i, _ in moves: i.start()
    for i, o in moves:
        i.wait()
        o.start()
    for _, o in moves: o.wait()

def deliver_call(*vals):
    HB = pl.BlockSpec(memory_space=pl.ANY)
    return pl.pallas_call(deliver, in_specs=[HB] * 3, out_specs=[HB] * 3,
        out_shape=[jax.ShapeDtypeStruct(v.shape, F32) for v in vals],
        scratch_shapes=[pltpu.VMEM(v.shape, F32) for v in vals] + [pltpu.SemaphoreType.DMA((sum(PARTS),))] * 2,
        compiler_params=pltpu.CompilerParams(vmem_limit_bytes=60 << 20))(*vals)

def solution(mesh):
    call = make_kernel(mesh.shape["row"])
    def body(panel, trailing):
        return tuple(deliver_call(*call(panel, trailing)))
    return jax.shard_map(body, mesh=mesh, in_specs=(P("col", "row"), P("row", "col")),
                         out_specs=(P(), P(None, "col"), P("row", "col")), check_vma=False)
```

```python
import jax
import jax.numpy as jnp
from jax import lax
from jax.experimental import pallas as pl
from jax.experimental.pallas import tpu as pltpu
from jax.sharding import PartitionSpec as P

MESH = pl.DeviceIdType.MESH
K = 4096
H = K // 2
S1P, S1M, F1P, F1M = 0, 1, 2, 3
S2P, S2M, F2P, F2M = 4, 9, 14, 18
NMSG = 22

class Half:
    def __init__(self, half, panel, g, ssem, rsem, x, y):
        self.h, self.panel, self.g, self.ss, self.rs = half, panel, g, ssem, rsem
        self.p, self.q = (x, y) if half == 0 else (y, x)
        w = lambda v: lax.rem(v, 4)
        self.P = [self.p, w(self.p + 3), w(self.p + 1), w(self.p + 2)]
        self.Q = [self.q, w(self.q + 3), w(self.q + 1), w(self.q + 2)]
        self.pending = []
    def col(self, p, q):
        return p * 4 + q if self.h == 0 else q * 4 + p
    def slc(self, p, q, lo, n):
        r = pl.multiple_of(self.col(p, q) * 16 + 8 * self.h, 8)
        return self.g.at[pl.ds(r, 8), pl.ds(lo, n)]
    def send(self, m, p, q, lo, n, axis, sign, own=False):
        dst = self.slc(p, q, lo, n)
        src = self.panel.at[pl.ds(8 * self.h, 8), pl.ds(lo, n)] if own else dst
        i = 1 if sign < 0 else 2
        to = self.col(self.P[i], self.q) if axis == 1 else self.col(self.p, self.Q[i])
        c = pltpu.make_async_remote_copy(src, dst, self.ss.at[self.h, m], self.rs.at[self.h, m], device_id={"col": to}, device_id_type=MESH)
        c.start()
        self.pending.append(c)
    def recv(self, m, p, q, lo, n):
        d = self.slc(p, q, lo, n)
        pltpu.make_async_remote_copy(d, d, self.ss.at[self.h, m], self.rs.at[self.h, m], device_id={"col": self.col(self.P[1], self.q)}, device_id_type=MESH).wait_recv()
    def start_own(self):
        self.send(S1P, self.p, self.q, 0, K, 1, 1, True)
        self.send(S1M, self.p, self.q, 0, K, 1, -1, True)
    def start_own2(self):
        self.send(S2P, self.p, self.q, 0, K, 2, 1, True)
        self.send(S2M, self.p, self.q, 0, K, 2, -1, True)
    def first_p(self):
        pm = self.P[1]
        self.recv(S1P, pm, self.q, 0, K)
        self.send(F1P, pm, self.q, 0, H, 1, 1)
        self.send(S2P + 1, pm, self.q, 0, K, 2, 1)
        self.send(S2M + 1, pm, self.q, 0, K, 2, -1)
    def first_m(self):
        pp = self.P[2]
        self.recv(S1M, pp, self.q, 0, K)
        self.send(F1M, pp, self.q, H, H, 1, -1)
        self.send(S2P + 2, pp, self.q, 0, K, 2, 1)
        self.send(S2M + 2, pp, self.q, 0, K, 2, -1)
    def far(self):
        po = self.P[3]
        self.recv(F1P, po, self.q, 0, H)
        self.send(S2P + 3, po, self.q, 0, H, 2, 1)
        self.send(S2M + 3, po, self.q, 0, H, 2, -1)
        self.recv(F1M, po, self.q, H, H)
        self.send(S2P + 4, po, self.q, H, H, 2, 1)
        self.send(S2M + 4, po, self.q, H, H, 2, -1)
    def second(self, s):
        ps = self.P[s]
        if s < 3:
            self.recv(S2P + s, ps, self.Q[1], 0, K)
            self.send(F2P + s, ps, self.Q[1], 0, H, 2, 1)
            self.recv(S2M + s, ps, self.Q[2], 0, K)
            self.send(F2M + s, ps, self.Q[2], H, H, 2, -1)
        else:
            self.recv(S2P + 3, ps, self.Q[1], 0, H)
            self.send(F2P + 3, ps, self.Q[1], 0, H, 2, 1)
            self.recv(S2M + 3, ps, self.Q[2], 0, H)
            self.recv(S2P + 4, ps, self.Q[1], H, H)
            self.recv(S2M + 4, ps, self.Q[2], H, H)
            self.send(F2M + 3, ps, self.Q[2], H, H, 2, -1)
    def last(self, s):
        ps, qo = self.P[s], self.Q[3]
        self.recv(F2P + s, ps, qo, 0, H)
        self.recv(F2M + s, ps, qo, H, H)


HI = lax.Precision.HIGHEST
T = 16
N = 128

def dot(a, b, ca=1, cb=0):
    return lax.dot_general(a, b, (((ca,), (cb,)), ((), ())), precision=HI, preferred_element_type=jnp.float32)

def factor_steps(tiles, put):
    n = len(tiles)
    sub = lax.broadcasted_iota(jnp.int32, (T, N), 0)
    lane = lax.broadcasted_iota(jnp.int32, (T, N), 1)
    bl = lambda x, c: jnp.broadcast_to(x[:, c:c + 1], (T, N))
    bs = lambda x, r: jnp.broadcast_to(x[r:r + 1, :], (T, N))
    tiles = list(tiles)
    for k in range(n):
        t = tiles[k]
        inb = (lane >= T * k) & (lane < T * k + T)
        eye = jnp.where(lane - T * k == sub, 1.0, 0.0)
        cols = [bl(t, T * k + m) for m in range(T)]
        z = jnp.where(inb, eye, t)
        u = t
        li = z
        dinv = jnp.zeros((T, N), jnp.float32)
        drs = jnp.zeros((T, N), jnp.float32)
        piv = bs(cols[0], 0)
        for j in range(T):
            r = 1.0 / piv
            cj = jnp.where(sub == j, 0.0, cols[j])
            cl = jnp.where(sub > j, cols[j], 0.0)
            nxt = None
            if j + 1 < T:
                nxt = bs(cols[j + 1], j + 1) - (bs(cols[j], j + 1) * bs(cols[j + 1], j)) * r
            for m in range(j + 1, T):
                cols[m] = cols[m] - (cj * bs(cols[m], j)) * r
            dinv = jnp.where(sub == j, r, dinv)
            drs = jnp.where(sub == j, lax.rsqrt(piv), drs)
            zj = bs(z, j)
            li = jnp.where(sub == j, zj, li)
            u = u - (cl * bs(u, j)) * r
            z = z - (cj * zj) * r
            piv = nxt
        z = z * dinv
        row = sub + T * k
        put(k, jnp.where(lane >= row, u * drs, 0.0), jnp.where(lane <= row, li * drs, 0.0))
        zr = [bs(z, m) for m in range(T)]
        if k + 1 < n:
            ti = tiles[k + 1]
            c = [bl(ti, T * k + m) for m in range(T)]
            p = [c[m] * zr[m] for m in range(T)]
            while len(p) > 1:
                p = [p[a] + p[a + 1] for a in range(0, len(p), 2)]
            tiles[k + 1] = jnp.where(inb, 0.0, ti) - p[0]
        if k + 2 < n:
            low = jnp.concatenate(tiles[k + 2:], axis=0)
            d = dot(low[:, T * k:T * k + T], z)
            for i in range(k + 2, n):
                tiles[i] = jnp.where(inb, 0.0, tiles[i]) - d[T * (i - k - 2):T * (i - k - 1)]
        yield k


NC = 16
F32 = jnp.float32
BF = jnp.bfloat16
ORDER = ("gr own own2 sp",
         "gl gp fp fm",
         "gpl s0 far s1",
         "s2 ow p1 s3",
         "ga sc1 l0 l1",
         "l2 l3 p2 gc",
         "sc2 gd f f",
         "sp1 sp2 f f",
         "f bk1 f f",
         "bk2 f e1 e2",
         "up")
CUT = 160
LIMIT = 60 << 20

def split(v):
    hi = v.astype(BF)
    return hi, (v - hi.astype(F32)).astype(BF)

def make_kernel(NR, order=ORDER):
    NZ = NR // 2
    def kernel(panel, trail, r_out, top_out, upd,
               g, li, ssem, rsem, lsem, us, xb, tr, t2, gp3, gx, rs16, zb, gall, pp, px, prs, q1, q2, pall, pn, qs, qr):
        c = lax.axis_index("col")
        w = lax.axis_index("row")
        x, y = c // 4, lax.rem(c, 4)
        z, core = w // 2, lax.rem(w, 2)
        sib = {"row": z * 2 + 1 - core}
        far = lambda i, n: min(i, n - i)
        steps_c = sorted(((a, b) for a in range(4) for b in range(4) if a + b), key=lambda v: -far(v[0], 4) - far(v[1], 4))
        cols = [lax.rem(x + a, 4) * 4 + lax.rem(y + b, 4) for a, b in steps_c]
        zs = [lax.rem(z + i, NZ) for i in sorted(range(1, NZ), key=lambda i: -far(i, NZ))]
        own = pltpu.make_async_copy(panel, g.at[pl.ds(pl.multiple_of(c * 16, 16), 16), :], lsem.at[0])
        own.start()
        mine = pltpu.make_async_copy(panel.at[:, pl.ds(pl.multiple_of(c * 256, 256), 256)], xb.at[pl.ds(pl.multiple_of(c * 16, 16), 16), :], lsem.at[1])
        mine.start()
        tcopy = pltpu.make_async_copy(trail, tr, lsem.at[2])
        tcopy.start()
        A = Half(0, panel, g, ssem, rsem, x, y)
        B = Half(1, panel, g, ssem, rsem, x, y)
        bar = pltpu.get_barrier_semaphore()
        for j in zs:
            for k in range(2):
                pl.semaphore_signal(bar, inc=1, device_id={"row": j * 2 + k}, device_id_type=MESH)
        pl.semaphore_signal(bar, inc=1, device_id=sib, device_id_type=MESH)
        for j in cols:
            pl.semaphore_signal(bar, inc=1, device_id={"col": j}, device_id_type=MESH)
        pl.semaphore_wait(bar, NC + NR - 2)

        def send(k, src, dst, dev):
            pltpu.make_async_remote_copy(src, dst, qs.at[k], qr.at[k], device_id=dev, device_id_type=MESH).start()
        def got(k, ref, sent=False):
            d = pltpu.make_async_remote_copy(ref, ref, qs.at[k], qr.at[k], device_id=sib, device_id_type=MESH)
            d.wait_send() if sent else d.wait_recv()

        def g_rows():
            for j in cols:
                send(0, panel.at[:, pl.ds(pl.multiple_of(j * 256, 256), 256)], xb.at[pl.ds(pl.multiple_of(c * 16, 16), 16), :], {"col": j})
        def g_local():
            mine.wait()
            got(0, xb.at[pl.ds(0, 240), :])
            hi = xb[:128, :]
            xv = xb[...]
            top = dot(hi, xv, 1, 1)
            low = dot(xb[128:, :], xb[128:, :], 1, 1)
            gp3[pl.ds(0, 128), 0, :] = top[:, :128]
            gp3[pl.ds(128, 128), 0, :] = top[:, 128:]
            gp3[pl.ds(256, 128), 0, :] = low
            send(1, gp3.at[pl.ds((1 - core) * 192, 192)], gx, sib)
        def g_pair():
            got(1, gx)
            gx[...] += gp3[pl.ds(core * 192, 192)]
            for i, j in enumerate(cols):
                send(2, gx.at[pl.ds(j * 12, 12)], rs16.at[pl.ds(i * 12, 12)], {"col": j})
        def g_plane():
            got(2, rs16)
            acc = gx[pl.ds(c * 12, 12)]
            for i in range(NC - 1):
                acc = acc + rs16[pl.ds(i * 12, 12)]
            zb[pl.ds(z * 12, 12)] = acc
            for j in zs:
                send(3, zb.at[pl.ds(z * 12, 12)], zb.at[pl.ds(z * 12, 12)], {"row": j * 2 + core})
        def g_all():
            got(3, zb.at[pl.ds(0, 12 * (NZ - 1))])
            acc = zb[pl.ds(0, 12)]
            for i in range(1, NZ):
                acc = acc + zb[pl.ds(i * 12, 12)]
            at = pl.ds(core * 192 + c * 12, 12)
            gall[at] = acc
            for j in cols:
                send(4, gall.at[at], gall.at[at], {"col": j})
        def g_cols():
            got(4, gall.at[pl.ds(0, 180)])
            at = pl.ds(core * 192, 192)
            send(5, gall.at[at], gall.at[at], sib)
        def g_done():
            got(5, gall.at[pl.ds(0, 192)])

        early = [(t, q) for t in range(4) for q in range(3) if t < 3 or q == 0]
        late = [(t, q) for t in range(4) for q in range(4) if (t, q) not in early]
        tiles = [(hf, t, q) for t, q in early + late for hf in (A, B)]
        rows = [pl.multiple_of(16 * hf.col(hf.P[t], hf.Q[q]) + 8 * hf.h, 8) for hf, t, q in tiles]
        base = (0, CUT, 256)
        CH, PC = 512, 1024
        def p_local(i):
            lo, hi_ = base[i], base[i + 1]
            m = hi_ - lo
            mine_ = rows[lo // 8:hi_ // 8]
            def step(n, acc):
                k0 = pl.multiple_of(n * PC, PC)
                v = jnp.concatenate([g[pl.ds(r, 8), pl.ds(k0, PC)] for r in mine_], axis=0)
                hi, l = split(v)
                return acc + jnp.dot(jnp.concatenate([hi, l], axis=0), t2[pl.ds(k0, PC), :], preferred_element_type=F32)
            acc = lax.fori_loop(0, K // PC, step, jnp.zeros((2 * m, 256), F32))
            pp[pl.ds(lo, m), 0, :] = ((acc[m:, 128:] + acc[:m, 128:]) + acc[m:, :128]) + acc[:m, :128]
            h = m // 2
            send(6 + 4 * i, pp.at[pl.ds(lo + (1 - core) * h, h)], px.at[pl.ds(lo // 2, h)], sib)
        def p_pair(i):
            lo, h = base[i], (base[i + 1] - base[i]) // 2
            at = pl.ds(lo // 2, h)
            got(6 + 4 * i, px.at[at])
            return at, px[at] + pp[pl.ds(lo + core * h, h)]
        def sizes(i):
            h = (base[i + 1] - base[i]) // 2
            u = h // NZ
            return base[i], h, u, (NZ - 1) * base[i] // (2 * NZ)
        LH = (256 - CUT) // 2
        Q = min(4, NZ)
        NG = NZ // Q
        zq, zg = lax.rem(z, Q), z // Q
        def q_near():
            _, v = p_pair(1)
            at = pl.ds(zq * LH, LH)
            q1[at] = v
            for i in sorted(range(1, Q), key=lambda i: -far(i, Q)):
                send(11, q1.at[at], q1.at[at], {"row": (zg * Q + lax.rem(zq + i, Q)) * 2 + core})
        def total(ref, n):
            acc = ref[pl.ds(0, LH)]
            for i in range(1, n):
                acc = acc + ref[pl.ds(i * LH, LH)]
            return acc
        def q_far():
            got(11, q1.at[pl.ds(0, (Q - 1) * LH)])
            at = pl.ds(zg * LH, LH)
            q2[at] = total(q1, Q)
            for i in sorted(range(1, NG), key=lambda i: -far(i, NG)):
                send(12, q2.at[at], q2.at[at], {"row": (lax.rem(zg + i, NG) * Q + zq) * 2 + core})
        def q_back():
            if NG > 1:
                got(12, q2.at[pl.ds(0, (NG - 1) * LH)])
            at = pl.ds(CUT + core * LH, LH)
            pall[at] = total(q2, NG)
            send(13, pall.at[at], pall.at[at], sib)
        def p_scatter(i):
            lo, h, u, o = sizes(i)
            at, v = p_pair(i)
            px[at] = v
            for n, j in enumerate(zs):
                send(7 + 4 * i, px.at[pl.ds(lo // 2 + j * u, u)], prs.at[pl.ds(o + n * u, u)], {"row": j * 2 + core})
        def p_spread(i):
            lo, h, u, o = sizes(i)
            got(7 + 4 * i, prs.at[pl.ds(o, (NZ - 1) * u)])
            acc = px[pl.ds(lo // 2 + z * u, u)]
            for n in range(NZ - 1):
                acc = acc + prs[pl.ds(o + n * u, u)]
            at = pl.ds(lo + core * h + z * u, u)
            pall[at] = acc
            for j in zs:
                send(8 + 4 * i, pall.at[at], pall.at[at], {"row": j * 2 + core})
        def p_back(i):
            lo, h, u, o = sizes(i)
            got(8 + 4 * i, pall.at[pl.ds(0, (NZ - 1) * u)])
            at = pl.ds(lo + core * h, h)
            send(9 + 4 * i, pall.at[at], pall.at[at], sib)
        def p_end(i):
            lo, h, u, o = sizes(i)
            got(9 + 4 * i, pall.at[pl.ds(0, h)])
            for t in range(h // 4):
                pn[pl.ds(rows[lo // 8 + t], 8), :] = pall[pl.ds(lo + 8 * t, 8), 0, :]
        def p_sent():
            lo, h, u, o = sizes(0)
            got(6, px.at[pl.ds(0, h)], True)
            got(7, prs, True)
            got(8, pall.at[pl.ds(0, (NZ - 1) * u)], True)
            got(9, pall.at[pl.ds(0, h)], True)
            got(10, px.at[pl.ds(0, LH)], True)
            got(11, q1.at[pl.ds(0, (Q - 1) * LH)], True)
            if NG > 1:
                got(12, q2.at[pl.ds(0, (NG - 1) * LH)], True)
            got(13, pall.at[pl.ds(0, LH)], True)

        def put_at(o):
            def put(k, rt, lt):
                r_out[o + 16 * k:o + 16 * k + 16, o:o + 128] = rt
                li[o + 16 * k:o + 16 * k + 16, o:o + 128] = lt
            return put
        def factor():
            for k in factor_steps([gall[pl.ds(16 * i, 16), 0, :] for i in range(8)], put_at(0)):
                if k % 2 == 1: yield
            linv1 = li[:128, :128]
            r12 = dot(linv1, gall[pl.ds(128, 128), 0, :])
            r_out[:128, 128:] = r12
            r_out[128:, :128] = jnp.zeros((128, 128), F32)
            li[:128, 128:] = jnp.zeros((128, 128), F32)
            s = gall[pl.ds(256, 128), 0, :] - dot(r12, r12, 0, 0)
            for k in factor_steps([s[16 * i:16 * i + 16, :] for i in range(8)], put_at(128)):
                if k == 7:
                    li[128:, :128] = -dot(li[128:, 128:], dot(r12, linv1, 0, 0))
                    xb[...] = dot(li[...], li[...], 0, 0)
                if k % 2 == 1: yield
        steps = factor()
        def update():
            p = pn[...]
            hi, lo = split(dot(p, xb[...], 0, 0))
            cf = jnp.concatenate([hi, lo], axis=0)
            top_out[...] = dot(li[...], p)
            for n in range(K // CH):
                at = pl.ds(n * CH, CH)
                hi, lo = split(g[:, at])
                a = jnp.dot(cf, hi, preferred_element_type=F32)
                b = jnp.dot(cf, lo, preferred_element_type=F32)
                v = ((b[128:] + a[128:]) + b[:128]) + a[:128]
                tr[at, :] -= v.T
                pltpu.make_async_copy(tr.at[at, :], upd.at[at, :], us.at[n]).start()
            for n in range(K // CH):
                at = pl.ds(n * CH, CH)
                pltpu.make_async_copy(tr.at[at, :], upd.at[at, :], us.at[n]).wait()
        def split_trail():
            tcopy.wait()
            @pl.loop(0, K // CH)
            def _(i):
                at = pl.ds(pl.multiple_of(i * CH, CH), CH)
                hi, lo = split(tr[at, :])
                t2[at, :128] = hi
                t2[at, 128:] = lo

        def both(name, *a):
            for hf in (A, B):
                getattr(hf, name)(*a)
        def adv(n):
            for _ in range(n): next(steps, None)
        do = {"gr": g_rows, "gl": g_local, "gp": g_pair, "gpl": g_plane, "ga": g_all, "gc": g_cols, "gd": g_done, "sp": split_trail,
              "own": lambda: both("start_own"), "own2": lambda: both("start_own2"), "fp": lambda: both("first_p"), "fm": lambda: both("first_m"), "far": lambda: both("far"),
              "s0": lambda: both("second", 0), "s1": lambda: both("second", 1), "s2": lambda: both("second", 2), "s3": lambda: both("second", 3),
              "l0": lambda: both("last", 0), "l1": lambda: both("last", 1), "l2": lambda: both("last", 2), "l3": lambda: both("last", 3),
              "p1": lambda: p_local(0), "p2": lambda: p_local(1), "sc1": lambda: p_scatter(0), "sp1": lambda: p_spread(0), "bk1": lambda: p_back(0), "e1": lambda: p_end(0),
              "sc2": q_near, "sp2": q_far, "bk2": q_back, "e2": lambda: p_end(1),
              "up": update, "ow": own.wait,
              "f": lambda: adv(1)}
        todo = [w for l in order for w in l.split()]
        for nm in todo:
            do[nm]()
        if "gl" not in todo:
            mine.wait()
        if "ow" not in todo:
            own.wait()
        if "sp" not in todo:
            tcopy.wait()
        for q in A.pending + B.pending:
            q.wait_send()
        if "gr" in todo:
            got(0, xb.at[pl.ds(0, 240), :], True)
            got(1, gx, True)
            got(2, rs16, True)
            got(3, zb.at[pl.ds(0, 12 * (NZ - 1))], True)
            got(4, gall.at[pl.ds(0, 180)], True)
            got(5, gall.at[pl.ds(0, 192)], True)
        if "p1" in todo:
            p_sent()
    V = pl.BlockSpec(memory_space=pltpu.VMEM)
    HB = pl.BlockSpec(memory_space=pltpu.HBM)
    def call(panel, trail):
        sh = lambda *s: jax.ShapeDtypeStruct(s, F32)
        vm = lambda *s: pltpu.VMEM(s, F32)
        return pl.pallas_call(kernel,
            out_shape=[sh(256, 256), sh(256, 128), sh(K, 128)],
            in_specs=[HB, HB], out_specs=[V, V, HB],
            scratch_shapes=[vm(256, K), vm(256, 256), pltpu.SemaphoreType.DMA((2, NMSG)), pltpu.SemaphoreType.DMA((2, NMSG)), pltpu.SemaphoreType.DMA((3,)), pltpu.SemaphoreType.DMA((8,)),
                vm(256, 256), vm(K, 128), pltpu.VMEM((K, 256), BF),
                vm(384, 1, 128), vm(192, 1, 128), vm(180, 1, 128), vm(12 * NZ, 1, 128), vm(384, 1, 128),
                vm(256, 1, 128), vm(128, 1, 128), vm(CUT // 2 * (NZ - 1) // NZ, 1, 128), vm(128 - CUT // 2 << 2, 1, 128), vm(128 - CUT // 2 << 2, 1, 128), vm(256, 1, 128), vm(256, 128),
                pltpu.SemaphoreType.DMA((14,)), pltpu.SemaphoreType.DMA((14,))],
            compiler_params=pltpu.CompilerParams(collective_id=0, has_side_effects=True, vmem_limit_bytes=LIMIT))(panel, trail)
    return call

PARTS = (1, 1, 4)
def deliver(a, b, c, a_out, b_out, c_out, a_buf, b_buf, c_buf, si, so):
    moves = []
    for src, buf, dst, parts in ((c, c_buf, c_out, PARTS[2]), (a, a_buf, a_out, PARTS[0]), (b, b_buf, b_out, PARTS[1])):
        n = src.shape[0] // parts
        for i in range(parts):
            at, k = pl.ds(i * n, n), len(moves)
            moves.append((pltpu.make_async_copy(src.at[at, :], buf.at[at, :], si.at[k]), pltpu.make_async_copy(buf.at[at, :], dst.at[at, :], so.at[k])))
    for i, _ in moves: i.start()
    for i, o in moves:
        i.wait()
        o.start()
    for _, o in moves: o.wait()

def deliver_call(*vals):
    HB = pl.BlockSpec(memory_space=pl.ANY)
    return pl.pallas_call(deliver, in_specs=[HB] * 3, out_specs=[HB] * 3,
        out_shape=[jax.ShapeDtypeStruct(v.shape, F32) for v in vals],
        scratch_shapes=[pltpu.VMEM(v.shape, F32) for v in vals] + [pltpu.SemaphoreType.DMA((sum(PARTS),))] * 2,
        compiler_params=pltpu.CompilerParams(vmem_limit_bytes=60 << 20))(*vals)

def solution(mesh):
    call = make_kernel(mesh.shape["row"])
    def body(panel, trailing):
        return tuple(deliver_call(*call(panel, trailing)))
    return jax.shard_map(body, mesh=mesh, in_specs=(P("col", "row"), P("row", "col")),
                         out_specs=(P(), P(None, "col"), P("row", "col")), check_vma=False)
```

```python
import jax
import jax.numpy as jnp
from jax import lax
from jax.experimental import pallas as pl
from jax.experimental.pallas import tpu as pltpu
from jax.sharding import PartitionSpec as P

MESH = pl.DeviceIdType.MESH
K = 4096
H = K // 2
S1P, S1M, F1P, F1M = 0, 1, 2, 3
S2P, S2M, F2P, F2M = 4, 9, 14, 18
NMSG = 22

class Half:
    def __init__(self, half, panel, g, ssem, rsem, x, y):
        self.h, self.panel, self.g, self.ss, self.rs = half, panel, g, ssem, rsem
        self.p, self.q = (x, y) if half == 0 else (y, x)
        w = lambda v: lax.rem(v, 4)
        self.P = [self.p, w(self.p + 3), w(self.p + 1), w(self.p + 2)]
        self.Q = [self.q, w(self.q + 3), w(self.q + 1), w(self.q + 2)]
        self.pending = []
    def col(self, p, q):
        return p * 4 + q if self.h == 0 else q * 4 + p
    def slc(self, p, q, lo, n):
        r = pl.multiple_of(self.col(p, q) * 16 + 8 * self.h, 8)
        return self.g.at[pl.ds(r, 8), pl.ds(lo, n)]
    def send(self, m, p, q, lo, n, axis, sign, own=False):
        dst = self.slc(p, q, lo, n)
        src = self.panel.at[pl.ds(8 * self.h, 8), pl.ds(lo, n)] if own else dst
        i = 1 if sign < 0 else 2
        to = self.col(self.P[i], self.q) if axis == 1 else self.col(self.p, self.Q[i])
        c = pltpu.make_async_remote_copy(src, dst, self.ss.at[self.h, m], self.rs.at[self.h, m], device_id={"col": to}, device_id_type=MESH)
        c.start()
        self.pending.append(c)
    def recv(self, m, p, q, lo, n):
        d = self.slc(p, q, lo, n)
        pltpu.make_async_remote_copy(d, d, self.ss.at[self.h, m], self.rs.at[self.h, m], device_id={"col": self.col(self.P[1], self.q)}, device_id_type=MESH).wait_recv()
    def start_own(self):
        self.send(S1P, self.p, self.q, 0, K, 1, 1, True)
        self.send(S1M, self.p, self.q, 0, K, 1, -1, True)
    def start_own2(self):
        self.send(S2P, self.p, self.q, 0, K, 2, 1, True)
        self.send(S2M, self.p, self.q, 0, K, 2, -1, True)
    def first_p(self):
        pm = self.P[1]
        self.recv(S1P, pm, self.q, 0, K)
        self.send(F1P, pm, self.q, 0, H, 1, 1)
        self.send(S2P + 1, pm, self.q, 0, K, 2, 1)
        self.send(S2M + 1, pm, self.q, 0, K, 2, -1)
    def first_m(self):
        pp = self.P[2]
        self.recv(S1M, pp, self.q, 0, K)
        self.send(F1M, pp, self.q, H, H, 1, -1)
        self.send(S2P + 2, pp, self.q, 0, K, 2, 1)
        self.send(S2M + 2, pp, self.q, 0, K, 2, -1)
    def far(self):
        po = self.P[3]
        self.recv(F1P, po, self.q, 0, H)
        self.send(S2P + 3, po, self.q, 0, H, 2, 1)
        self.send(S2M + 3, po, self.q, 0, H, 2, -1)
        self.recv(F1M, po, self.q, H, H)
        self.send(S2P + 4, po, self.q, H, H, 2, 1)
        self.send(S2M + 4, po, self.q, H, H, 2, -1)
    def second(self, s):
        ps = self.P[s]
        if s < 3:
            self.recv(S2P + s, ps, self.Q[1], 0, K)
            self.send(F2P + s, ps, self.Q[1], 0, H, 2, 1)
            self.recv(S2M + s, ps, self.Q[2], 0, K)
            self.send(F2M + s, ps, self.Q[2], H, H, 2, -1)
        else:
            self.recv(S2P + 3, ps, self.Q[1], 0, H)
            self.send(F2P + 3, ps, self.Q[1], 0, H, 2, 1)
            self.recv(S2M + 3, ps, self.Q[2], 0, H)
            self.recv(S2P + 4, ps, self.Q[1], H, H)
            self.recv(S2M + 4, ps, self.Q[2], H, H)
            self.send(F2M + 3, ps, self.Q[2], H, H, 2, -1)
    def last(self, s):
        ps, qo = self.P[s], self.Q[3]
        self.recv(F2P + s, ps, qo, 0, H)
        self.recv(F2M + s, ps, qo, H, H)


HI = lax.Precision.HIGHEST
T = 16
N = 128

def dot(a, b, ca=1, cb=0):
    return lax.dot_general(a, b, (((ca,), (cb,)), ((), ())), precision=HI, preferred_element_type=jnp.float32)

def factor_steps(tiles, put):
    n = len(tiles)
    sub = lax.broadcasted_iota(jnp.int32, (T, N), 0)
    lane = lax.broadcasted_iota(jnp.int32, (T, N), 1)
    bl = lambda x, c: jnp.broadcast_to(x[:, c:c + 1], (T, N))
    bs = lambda x, r: jnp.broadcast_to(x[r:r + 1, :], (T, N))
    tiles = list(tiles)
    for k in range(n):
        t = tiles[k]
        inb = (lane >= T * k) & (lane < T * k + T)
        eye = jnp.where(lane - T * k == sub, 1.0, 0.0)
        cols = [bl(t, T * k + m) for m in range(T)]
        z = jnp.where(inb, eye, t)
        u = t
        li = z
        dinv = jnp.zeros((T, N), jnp.float32)
        drs = jnp.zeros((T, N), jnp.float32)
        piv = bs(cols[0], 0)
        for j in range(T):
            r = 1.0 / piv
            cj = jnp.where(sub == j, 0.0, cols[j])
            cl = jnp.where(sub > j, cols[j], 0.0)
            nxt = None
            if j + 1 < T:
                nxt = bs(cols[j + 1], j + 1) - (bs(cols[j], j + 1) * bs(cols[j + 1], j)) * r
            for m in range(j + 1, T):
                cols[m] = cols[m] - (cj * bs(cols[m], j)) * r
            dinv = jnp.where(sub == j, r, dinv)
            drs = jnp.where(sub == j, lax.rsqrt(piv), drs)
            zj = bs(z, j)
            li = jnp.where(sub == j, zj, li)
            u = u - (cl * bs(u, j)) * r
            z = z - (cj * zj) * r
            piv = nxt
        z = z * dinv
        row = sub + T * k
        put(k, jnp.where(lane >= row, u * drs, 0.0), jnp.where(lane <= row, li * drs, 0.0))
        zr = [bs(z, m) for m in range(T)]
        if k + 1 < n:
            ti = tiles[k + 1]
            c = [bl(ti, T * k + m) for m in range(T)]
            p = [c[m] * zr[m] for m in range(T)]
            while len(p) > 1:
                p = [p[a] + p[a + 1] for a in range(0, len(p), 2)]
            tiles[k + 1] = jnp.where(inb, 0.0, ti) - p[0]
        if k + 2 < n:
            low = jnp.concatenate(tiles[k + 2:], axis=0)
            d = dot(low[:, T * k:T * k + T], z)
            for i in range(k + 2, n):
                tiles[i] = jnp.where(inb, 0.0, tiles[i]) - d[T * (i - k - 2):T * (i - k - 1)]
        yield k


NC = 16
F32 = jnp.float32
BF = jnp.bfloat16
ORDER = ("gr own own2 sp",
         "gl gp fp fm",
         "gpl s0 far s1",
         "s2 ow p1 s3",
         "ga sc1 l0 l1",
         "l2 l3 p2 gc",
         "sc2 gd f f",
         "sp1 sp2 f f",
         "f bk1 f f",
         "bk2 f e1 e2",
         "up")
CUT = 160
LIMIT = 60 << 20

def split(v):
    hi = v.astype(BF)
    return hi, (v - hi.astype(F32)).astype(BF)

def make_kernel(NR, order=ORDER):
    NZ = NR // 2
    def kernel(panel, trail, r_out, top_out, upd,
               g, li, rv, tv, ssem, rsem, lsem, us, xb, tr, t2, gp3, gx, rs16, zb, gall, pp, px, prs, q1, q2, pall, pn, qs, qr):
        c = lax.axis_index("col")
        w = lax.axis_index("row")
        x, y = c // 4, lax.rem(c, 4)
        z, core = w // 2, lax.rem(w, 2)
        sib = {"row": z * 2 + 1 - core}
        far = lambda i, n: min(i, n - i)
        steps_c = sorted(((a, b) for a in range(4) for b in range(4) if a + b), key=lambda v: -far(v[0], 4) - far(v[1], 4))
        cols = [lax.rem(x + a, 4) * 4 + lax.rem(y + b, 4) for a, b in steps_c]
        zs = [lax.rem(z + i, NZ) for i in sorted(range(1, NZ), key=lambda i: -far(i, NZ))]
        own = pltpu.make_async_copy(panel, g.at[pl.ds(pl.multiple_of(c * 16, 16), 16), :], lsem.at[0])
        own.start()
        mine = pltpu.make_async_copy(panel.at[:, pl.ds(pl.multiple_of(c * 256, 256), 256)], xb.at[pl.ds(pl.multiple_of(c * 16, 16), 16), :], lsem.at[1])
        mine.start()
        tcopy = pltpu.make_async_copy(trail, tr, lsem.at[2])
        tcopy.start()
        A = Half(0, panel, g, ssem, rsem, x, y)
        B = Half(1, panel, g, ssem, rsem, x, y)
        bar = pltpu.get_barrier_semaphore()
        for j in zs:
            for k in range(2):
                pl.semaphore_signal(bar, inc=1, device_id={"row": j * 2 + k}, device_id_type=MESH)
        pl.semaphore_signal(bar, inc=1, device_id=sib, device_id_type=MESH)
        for j in cols:
            pl.semaphore_signal(bar, inc=1, device_id={"col": j}, device_id_type=MESH)
        pl.semaphore_wait(bar, NC + NR - 2)

        def send(k, src, dst, dev):
            pltpu.make_async_remote_copy(src, dst, qs.at[k], qr.at[k], device_id=dev, device_id_type=MESH).start()
        def got(k, ref, sent=False):
            d = pltpu.make_async_remote_copy(ref, ref, qs.at[k], qr.at[k], device_id=sib, device_id_type=MESH)
            d.wait_send() if sent else d.wait_recv()

        def g_rows():
            for j in cols:
                send(0, panel.at[:, pl.ds(pl.multiple_of(j * 256, 256), 256)], xb.at[pl.ds(pl.multiple_of(c * 16, 16), 16), :], {"col": j})
        def g_local():
            mine.wait()
            got(0, xb.at[pl.ds(0, 240), :])
            hi = xb[:128, :]
            xv = xb[...]
            top = dot(hi, xv, 1, 1)
            low = dot(xb[128:, :], xb[128:, :], 1, 1)
            gp3[pl.ds(0, 128), 0, :] = top[:, :128]
            gp3[pl.ds(128, 128), 0, :] = top[:, 128:]
            gp3[pl.ds(256, 128), 0, :] = low
            send(1, gp3.at[pl.ds((1 - core) * 192, 192)], gx, sib)
        def g_pair():
            got(1, gx)
            gx[...] += gp3[pl.ds(core * 192, 192)]
            for i, j in enumerate(cols):
                send(2, gx.at[pl.ds(j * 12, 12)], rs16.at[pl.ds(i * 12, 12)], {"col": j})
        def g_plane():
            got(2, rs16)
            acc = gx[pl.ds(c * 12, 12)]
            for i in range(NC - 1):
                acc = acc + rs16[pl.ds(i * 12, 12)]
            zb[pl.ds(z * 12, 12)] = acc
            for j in zs:
                send(3, zb.at[pl.ds(z * 12, 12)], zb.at[pl.ds(z * 12, 12)], {"row": j * 2 + core})
        def g_all():
            got(3, zb.at[pl.ds(0, 12 * (NZ - 1))])
            acc = zb[pl.ds(0, 12)]
            for i in range(1, NZ):
                acc = acc + zb[pl.ds(i * 12, 12)]
            at = pl.ds(core * 192 + c * 12, 12)
            gall[at] = acc
            for j in cols:
                send(4, gall.at[at], gall.at[at], {"col": j})
        def g_cols():
            got(4, gall.at[pl.ds(0, 180)])
            at = pl.ds(core * 192, 192)
            send(5, gall.at[at], gall.at[at], sib)
        def g_done():
            got(5, gall.at[pl.ds(0, 192)])

        early = [(t, q) for t in range(4) for q in range(3) if t < 3 or q == 0]
        late = [(t, q) for t in range(4) for q in range(4) if (t, q) not in early]
        tiles = [(hf, t, q) for t, q in early + late for hf in (A, B)]
        rows = [pl.multiple_of(16 * hf.col(hf.P[t], hf.Q[q]) + 8 * hf.h, 8) for hf, t, q in tiles]
        base = (0, CUT, 256)
        CH, PC = 512, 1024
        def p_local(i):
            lo, hi_ = base[i], base[i + 1]
            m = hi_ - lo
            mine_ = rows[lo // 8:hi_ // 8]
            def step(n, acc):
                k0 = pl.multiple_of(n * PC, PC)
                v = jnp.concatenate([g[pl.ds(r, 8), pl.ds(k0, PC)] for r in mine_], axis=0)
                hi, l = split(v)
                return acc + jnp.dot(jnp.concatenate([hi, l], axis=0), t2[pl.ds(k0, PC), :], preferred_element_type=F32)
            acc = lax.fori_loop(0, K // PC, step, jnp.zeros((2 * m, 256), F32))
            pp[pl.ds(lo, m), 0, :] = ((acc[m:, 128:] + acc[:m, 128:]) + acc[m:, :128]) + acc[:m, :128]
            h = m // 2
            send(6 + 4 * i, pp.at[pl.ds(lo + (1 - core) * h, h)], px.at[pl.ds(lo // 2, h)], sib)
        def p_pair(i):
            lo, h = base[i], (base[i + 1] - base[i]) // 2
            at = pl.ds(lo // 2, h)
            got(6 + 4 * i, px.at[at])
            return at, px[at] + pp[pl.ds(lo + core * h, h)]
        def sizes(i):
            h = (base[i + 1] - base[i]) // 2
            u = h // NZ
            return base[i], h, u, (NZ - 1) * base[i] // (2 * NZ)
        LH = (256 - CUT) // 2
        Q = min(4, NZ)
        NG = NZ // Q
        zq, zg = lax.rem(z, Q), z // Q
        def q_near():
            _, v = p_pair(1)
            at = pl.ds(zq * LH, LH)
            q1[at] = v
            for i in sorted(range(1, Q), key=lambda i: -far(i, Q)):
                send(11, q1.at[at], q1.at[at], {"row": (zg * Q + lax.rem(zq + i, Q)) * 2 + core})
        def total(ref, n):
            acc = ref[pl.ds(0, LH)]
            for i in range(1, n):
                acc = acc + ref[pl.ds(i * LH, LH)]
            return acc
        def q_far():
            got(11, q1.at[pl.ds(0, (Q - 1) * LH)])
            at = pl.ds(zg * LH, LH)
            q2[at] = total(q1, Q)
            for i in sorted(range(1, NG), key=lambda i: -far(i, NG)):
                send(12, q2.at[at], q2.at[at], {"row": (lax.rem(zg + i, NG) * Q + zq) * 2 + core})
        def q_back():
            if NG > 1:
                got(12, q2.at[pl.ds(0, (NG - 1) * LH)])
            at = pl.ds(CUT + core * LH, LH)
            pall[at] = total(q2, NG)
            send(13, pall.at[at], pall.at[at], sib)
        def p_scatter(i):
            lo, h, u, o = sizes(i)
            at, v = p_pair(i)
            px[at] = v
            for n, j in enumerate(zs):
                send(7 + 4 * i, px.at[pl.ds(lo // 2 + j * u, u)], prs.at[pl.ds(o + n * u, u)], {"row": j * 2 + core})
        def p_spread(i):
            lo, h, u, o = sizes(i)
            got(7 + 4 * i, prs.at[pl.ds(o, (NZ - 1) * u)])
            acc = px[pl.ds(lo // 2 + z * u, u)]
            for n in range(NZ - 1):
                acc = acc + prs[pl.ds(o + n * u, u)]
            at = pl.ds(lo + core * h + z * u, u)
            pall[at] = acc
            for j in zs:
                send(8 + 4 * i, pall.at[at], pall.at[at], {"row": j * 2 + core})
        def p_back(i):
            lo, h, u, o = sizes(i)
            got(8 + 4 * i, pall.at[pl.ds(0, (NZ - 1) * u)])
            at = pl.ds(lo + core * h, h)
            send(9 + 4 * i, pall.at[at], pall.at[at], sib)
        def p_end(i):
            lo, h, u, o = sizes(i)
            got(9 + 4 * i, pall.at[pl.ds(0, h)])
            for t in range(h // 4):
                pn[pl.ds(rows[lo // 8 + t], 8), :] = pall[pl.ds(lo + 8 * t, 8), 0, :]
        def p_sent():
            lo, h, u, o = sizes(0)
            got(6, px.at[pl.ds(0, h)], True)
            got(7, prs, True)
            got(8, pall.at[pl.ds(0, (NZ - 1) * u)], True)
            got(9, pall.at[pl.ds(0, h)], True)
            got(10, px.at[pl.ds(0, LH)], True)
            got(11, q1.at[pl.ds(0, (Q - 1) * LH)], True)
            if NG > 1:
                got(12, q2.at[pl.ds(0, (NG - 1) * LH)], True)
            got(13, pall.at[pl.ds(0, LH)], True)

        def put_at(o):
            def put(k, rt, lt):
                rv[o + 16 * k:o + 16 * k + 16, o:o + 128] = rt
                li[o + 16 * k:o + 16 * k + 16, o:o + 128] = lt
            return put
        def factor():
            for k in factor_steps([gall[pl.ds(16 * i, 16), 0, :] for i in range(8)], put_at(0)):
                if k % 2 == 1: yield
            linv1 = li[:128, :128]
            r12 = dot(linv1, gall[pl.ds(128, 128), 0, :])
            rv[:128, 128:] = r12
            rv[128:, :128] = jnp.zeros((128, 128), F32)
            li[:128, 128:] = jnp.zeros((128, 128), F32)
            s = gall[pl.ds(256, 128), 0, :] - dot(r12, r12, 0, 0)
            for k in factor_steps([s[16 * i:16 * i + 16, :] for i in range(8)], put_at(128)):
                if k == 7:
                    li[128:, :128] = -dot(li[128:, 128:], dot(r12, linv1, 0, 0))
                    rout.start()
                    xb[...] = dot(li[...], li[...], 0, 0)
                if k % 2 == 1: yield
        rout = pltpu.make_async_copy(rv, r_out, lsem.at[3])
        steps = factor()
        def update():
            p = pn[...]
            hi, lo = split(dot(p, xb[...], 0, 0))
            cf = jnp.concatenate([hi, lo], axis=0)
            for n in range(K // CH):
                at = pl.ds(n * CH, CH)
                hi, lo = split(g[:, at])
                a = jnp.dot(cf, hi, preferred_element_type=F32)
                b = jnp.dot(cf, lo, preferred_element_type=F32)
                v = ((b[128:] + a[128:]) + b[:128]) + a[:128]
                tr[at, :] -= v.T
                pltpu.make_async_copy(tr.at[at, :], upd.at[at, :], us.at[n]).start()
            tv[...] = dot(li[...], p)
            tout = pltpu.make_async_copy(tv, top_out, lsem.at[4])
            tout.start()
            for n in range(K // CH):
                at = pl.ds(n * CH, CH)
                pltpu.make_async_copy(tr.at[at, :], upd.at[at, :], us.at[n]).wait()
            rout.wait()
            tout.wait()
        def split_trail():
            tcopy.wait()
            @pl.loop(0, K // CH)
            def _(i):
                at = pl.ds(pl.multiple_of(i * CH, CH), CH)
                hi, lo = split(tr[at, :])
                t2[at, :128] = hi
                t2[at, 128:] = lo

        def both(name, *a):
            for hf in (A, B):
                getattr(hf, name)(*a)
        def adv(n):
            for _ in range(n): next(steps, None)
        do = {"gr": g_rows, "gl": g_local, "gp": g_pair, "gpl": g_plane, "ga": g_all, "gc": g_cols, "gd": g_done, "sp": split_trail,
              "own": lambda: both("start_own"), "own2": lambda: both("start_own2"), "fp": lambda: both("first_p"), "fm": lambda: both("first_m"), "far": lambda: both("far"),
              "s0": lambda: both("second", 0), "s1": lambda: both("second", 1), "s2": lambda: both("second", 2), "s3": lambda: both("second", 3),
              "l0": lambda: both("last", 0), "l1": lambda: both("last", 1), "l2": lambda: both("last", 2), "l3": lambda: both("last", 3),
              "p1": lambda: p_local(0), "p2": lambda: p_local(1), "sc1": lambda: p_scatter(0), "sp1": lambda: p_spread(0), "bk1": lambda: p_back(0), "e1": lambda: p_end(0),
              "sc2": q_near, "sp2": q_far, "bk2": q_back, "e2": lambda: p_end(1),
              "up": update, "ow": own.wait,
              "f": lambda: adv(1)}
        todo = [w for l in order for w in l.split()]
        for nm in todo:
            do[nm]()
        if "gl" not in todo:
            mine.wait()
        if "ow" not in todo:
            own.wait()
        if "sp" not in todo:
            tcopy.wait()
        for q in A.pending + B.pending:
            q.wait_send()
        if "gr" in todo:
            got(0, xb.at[pl.ds(0, 240), :], True)
            got(1, gx, True)
            got(2, rs16, True)
            got(3, zb.at[pl.ds(0, 12 * (NZ - 1))], True)
            got(4, gall.at[pl.ds(0, 180)], True)
            got(5, gall.at[pl.ds(0, 192)], True)
        if "p1" in todo:
            p_sent()
    HB = pl.BlockSpec(memory_space=pltpu.HBM)
    def call(panel, trail):
        sh = lambda *s: jax.ShapeDtypeStruct(s, F32)
        vm = lambda *s: pltpu.VMEM(s, F32)
        return pl.pallas_call(kernel,
            out_shape=[sh(256, 256), sh(256, 128), sh(K, 128)],
            in_specs=[HB, HB], out_specs=[HB, HB, HB],
            scratch_shapes=[vm(256, K), vm(256, 256), vm(256, 256), vm(256, 128), pltpu.SemaphoreType.DMA((2, NMSG)), pltpu.SemaphoreType.DMA((2, NMSG)), pltpu.SemaphoreType.DMA((5,)), pltpu.SemaphoreType.DMA((8,)),
                vm(256, 256), vm(K, 128), pltpu.VMEM((K, 256), BF),
                vm(384, 1, 128), vm(192, 1, 128), vm(180, 1, 128), vm(12 * NZ, 1, 128), vm(384, 1, 128),
                vm(256, 1, 128), vm(128, 1, 128), vm(CUT // 2 * (NZ - 1) // NZ, 1, 128), vm(128 - CUT // 2 << 2, 1, 128), vm(128 - CUT // 2 << 2, 1, 128), vm(256, 1, 128), vm(256, 128),
                pltpu.SemaphoreType.DMA((14,)), pltpu.SemaphoreType.DMA((14,))],
            compiler_params=pltpu.CompilerParams(collective_id=0, has_side_effects=True, vmem_limit_bytes=LIMIT))(panel, trail)
    return call

PARTS = (1, 1, 4)
def deliver(a, b, c, a_out, b_out, c_out, a_buf, b_buf, c_buf, si, so):
    moves = []
    for src, buf, dst, parts in ((c, c_buf, c_out, PARTS[2]), (a, a_buf, a_out, PARTS[0]), (b, b_buf, b_out, PARTS[1])):
        n = src.shape[0] // parts
        for i in range(parts):
            at, k = pl.ds(i * n, n), len(moves)
            moves.append((pltpu.make_async_copy(src.at[at, :], buf.at[at, :], si.at[k]), pltpu.make_async_copy(buf.at[at, :], dst.at[at, :], so.at[k])))
    for i, _ in moves: i.start()
    for i, o in moves:
        i.wait()
        o.start()
    for _, o in moves: o.wait()

def deliver_call(*vals):
    HB = pl.BlockSpec(memory_space=pl.ANY)
    return pl.pallas_call(deliver, in_specs=[HB] * 3, out_specs=[HB] * 3,
        out_shape=[jax.ShapeDtypeStruct(v.shape, F32) for v in vals],
        scratch_shapes=[pltpu.VMEM(v.shape, F32) for v in vals] + [pltpu.SemaphoreType.DMA((sum(PARTS),))] * 2,
        compiler_params=pltpu.CompilerParams(vmem_limit_bytes=60 << 20))(*vals)

def solution(mesh):
    call = make_kernel(mesh.shape["row"])
    def body(panel, trailing):
        return tuple(deliver_call(*call(panel, trailing)))
    return jax.shard_map(body, mesh=mesh, in_specs=(P("col", "row"), P("row", "col")),
                         out_specs=(P(), P(None, "col"), P("row", "col")), check_vma=False)
```
